128 devices in a mesh: mode: 4 (over z_lo, core), site: 32 (over y, z_hi, x).
Axes of the slice: x: 4, y: 4, z: 4 (z_hi: 2, z_lo: 2; z = z_hi * 2 + z_lo), core: 2. Of those that a mesh axis runs over, the one named last changes fastest.
Arguments:
- low_modes: bfloat16 [64, 4, 2, 3, 8, 65536], P('mode', None, None, None, None, 'site'), may hold values from -6 to 6
- high_modes: bfloat16 [64, 2, 3, 8, 65536], P('mode', None, None, None, 'site'), may hold values from -0.013671875 to 0.013671875
- pattern: int32 [64], replicated, may hold values from 0 to 3
- momenta: int32 [8, 3], replicated, may hold values from -2 to 2
Outputs:
- meson: float32 [4, 2, 64, 64, 64], P(None, None, 'site', None, 'mode')
The draws below stay inside these ranges and needn't reach their ends.
All inputs are finite; a program needn't handle non-finite values.
Results may differ from the reference program's by a relative error of at most 0.0065.
Values may be sent and summed in bfloat16 or wider, within the bound.
No kernel may reach another device: no remote copies, remote signals or barrier semaphores. Data moves between devices by JAX's collectives and lax.ppermute only.
A program may use at most 320 MiB of HBM per device.

```python
import math
import jax
import jax.numpy as jnp
import numpy as np
from jax import lax

LOW = 64
HIGH = 64
MOMS = 8
TW = 8
SPACE = 65536


def touch_ends(entries, rng, least, top_value):
    dims = entries.shape
    place = [jax.random.randint(jax.random.fold_in(rng, axis), (), 0, dims[axis]) for axis in range(len(dims))]
    entries = entries.at[tuple(place)].set(least)
    longest = dims.index(max(dims))
    place[longest] = (place[longest] + 1) % dims[longest]
    return entries.at[tuple(place)].set(top_value)


def level_of(key, shape, split, least, high):
    loudness, own = 1.0, jax.random.fold_in(key, 6)
    for dim, shards_of in split:
        heights = jnp.exp(jax.random.uniform(jax.random.fold_in(own, dim), (shards_of,), jnp.float32, least / len(split), high / len(split)))
        loudness = loudness * jnp.repeat(heights, shape[dim] // shards_of).reshape([-1 if axis == dim else 1 for axis in range(len(shape))])
    return loudness


def noise(key, extent, spread, limit, pieces=(), held_as=jnp.bfloat16):
    result = jax.random.normal(key, extent, jnp.float32) * spread
    if len(pieces) > 0:
        result = level_of(key, extent, pieces, -0.22, 0.18) * result
    return jnp.clip(result, min=-limit, max=limit).astype(held_as)


def setup_inputs(seed: int = 0) -> dict:
    seeds = jax.random.split(jax.random.key(seed), 5)
    low_modes = noise(seeds[0], (LOW, 4, 2, 3, TW, SPACE), 1.0, 6.0, ((0, 4), (5, 32)))
    high_modes = noise(seeds[1], (HIGH, 2, 3, TW, SPACE), (3 * SPACE) ** -0.5, 0.013671875, ((0, 4), (4, 32)))
    pattern = touch_ends(jax.random.randint(seeds[2], (HIGH,), 0, 4), jax.random.fold_in(seeds[2], 1), 0, 3).astype(jnp.int32)
    momenta = touch_ends(jax.random.randint(seeds[3], (MOMS, 3), -2, 3), jax.random.fold_in(seeds[3], 1), -2, 2).astype(jnp.int32)
    return dict(low_modes=low_modes, high_modes=high_modes, pattern=pattern, momenta=momenta)


def gamma_tables():
    real_table = np.zeros((4, 4, 4), np.float32)
    imag_table = np.zeros((4, 4, 4), np.float32)
    for spin in range(4):
        real_table[0, spin, spin] = 1.0
    for row_spin, col_spin in ((0, 2), (1, 3), (2, 0), (3, 1)):
        real_table[1, row_spin, col_spin] = 1.0
    for row_spin, col_spin, value in ((0, 3, 1.0), (1, 2, 1.0), (2, 1, -1.0), (3, 0, -1.0)):
        imag_table[2, row_spin, col_spin] = value
    for row_spin, col_spin, value in ((0, 1, -1.0), (1, 0, 1.0), (2, 3, -1.0), (3, 2, 1.0)):
        real_table[3, row_spin, col_spin] = value
    return real_table, imag_table


def phase_tables(momenta, first_site, count):
    sites = first_site + jnp.arange(count, dtype=jnp.int32)
    coords = jnp.stack([sites % 32, (sites // 32) % 32, sites // 1024])
    turns = jnp.sum(momenta[:, :, None] * coords[None, :, :], axis=1)
    angles = turns.astype(jnp.float32) * (2.0 * math.pi / 96.0)
    return jnp.cos(angles), jnp.sin(angles)


def reference(low_modes, high_modes, pattern, momenta):
    cosines, sines = phase_tables(momenta, 0, low_modes.shape[-1])
    real_table, imag_table = gamma_tables()
    select = (pattern[:, None] == jnp.arange(4, dtype=jnp.int32)[None, :]).astype(jnp.float32)
    coef_real = jnp.einsum("ha,gas->ghs", select, jnp.asarray(real_table, jnp.float32))
    coef_imag = jnp.einsum("ha,gas->ghs", select, jnp.asarray(imag_table, jnp.float32))

    def one_slice(slice_index):
        low_part = low_modes[:, :, :, :, slice_index, :].astype(jnp.float32)
        high_part = high_modes[:, :, :, slice_index, :].astype(jnp.float32)
        real_part = high_part[None, :, 0]
        imag_part = high_part[None, :, 1]
        cos_b = cosines[:, None, None, :]
        sin_b = sines[:, None, None, :]
        phased_real = real_part * cos_b - imag_part * sin_b
        phased_imag = real_part * sin_b + imag_part * cos_b
        phased = jnp.stack([phased_real, phased_imag], axis=2).astype(jnp.bfloat16)
        phased = lax.optimization_barrier(phased).astype(jnp.float32)
        products = jnp.einsum("phrcx,lsucx->phrlsu", phased, low_part)
        over_real = products[:, :, 0, :, :, 0] + products[:, :, 1, :, :, 1]
        over_imag = products[:, :, 0, :, :, 1] - products[:, :, 1, :, :, 0]
        meson_real = jnp.einsum("ghs,phls->gphl", coef_real, over_real) - jnp.einsum("ghs,phls->gphl", coef_imag, over_imag)
        meson_imag = jnp.einsum("ghs,phls->gphl", coef_real, over_imag) + jnp.einsum("ghs,phls->gphl", coef_imag, over_real)
        return jnp.stack([meson_real, meson_imag], axis=1)

    slices = lax.map(one_slice, jnp.arange(low_modes.shape[4], dtype=jnp.int32))
    ordered = jnp.transpose(slices, (1, 2, 0, 3, 4, 5))
    shape = ordered.shape
    return ordered.reshape(shape[0], shape[1], shape[2] * shape[3], shape[4], shape[5])
```

```python
import math

import jax
import jax.numpy as jnp
from jax import lax
from jax.experimental import pallas as pl
from jax.experimental.pallas import tpu as pltpu
from jax.sharding import PartitionSpec as P

NX, NY, NZ = 4, 4, 2
SLOTS = NY * NZ
PARTNER = ((0, 1, 2, 3), (2, 3, 0, 1), (3, 2, 1, 0), (1, 0, 3, 2))


def coords():
    site = lax.axis_index("site")
    return lax.rem(site, 4), lax.div(site, 8), lax.rem(lax.div(site, 4), 2)


def site_of(y, z, x):
    return ((y % NY) * NZ + z % NZ) * NX + x % NX


def move(block, dy, dz, dx):
    route = [
        (site_of(y, z, x), site_of(y + dy, z + dz, x + dx))
        for y in range(NY)
        for z in range(NZ)
        for x in range(NX)
    ]
    return lax.ppermute(block, "site", route)


def flip(block, mask):
    return lax.ppermute(block, "mode", [(i, i ^ mask) for i in range(4)])


def slot_of(t, y, z):
    distance = lax.rem(t // 2 - y + 2 * NY - 1, NY)
    same = 1 - jnp.abs(t % 2 - z)
    return same * NY + distance


def relayout_body(in_ref, out_ref):
    _, y, z = coords()
    rows = in_ref.shape[0]
    width = in_ref.shape[-1]
    lead = (0,) * (len(in_ref.shape) - 3)
    step = 512
    for j in range(0, width, step):
        values = in_ref[(slice(None),) + lead + (slice(None), pl.ds(j, step))].astype(jnp.float32)
        turned = jnp.swapaxes(values, 0, 1).astype(jnp.bfloat16)
        for t in range(SLOTS):
            out_ref[(slot_of(t, y, z),) + lead + (slice(None), pl.ds(j, step))] = turned[t]


def relayout_high(high):
    rows, two, colours, slices, count = high.shape
    return pl.pallas_call(
        relayout_body,
        grid=(two, colours),
        in_specs=[pl.BlockSpec((rows, 1, 1, slices, count), lambda r, c: (0, r, c, 0, 0))],
        out_specs=pl.BlockSpec((slices, 1, 1, rows, count), lambda r, c: (0, r, c, 0, 0)),
        out_shape=jax.ShapeDtypeStruct((slices, two, colours, rows, count), jnp.bfloat16),
        compiler_params=pltpu.CompilerParams(vmem_limit_bytes=16 * 2**20),
        cost_estimate=pl.CostEstimate(flops=0, bytes_accessed=2 * high.size * 2, transcendentals=0),
        name="relayout_high",
    )(high)


def relayout_low(low):
    rows, spins, two, colours, slices, count = low.shape
    return pl.pallas_call(
        relayout_body,
        grid=(colours, two, spins),
        in_specs=[
            pl.BlockSpec((rows, 1, 1, 1, slices, count), lambda c, u, s: (0, s, u, c, 0, 0))
        ],
        out_specs=pl.BlockSpec((slices, 1, 1, 1, rows, count), lambda c, u, s: (0, c, u, s, 0, 0)),
        out_shape=jax.ShapeDtypeStruct((slices, colours, two, spins, rows, count), jnp.bfloat16),
        compiler_params=pltpu.CompilerParams(vmem_limit_bytes=16 * 2**20),
        cost_estimate=pl.CostEstimate(flops=0, bytes_accessed=2 * low.size * 2, transcendentals=0),
        name="relayout_low",
    )(low)


def contract_body(pat_ref, cos_ref, sin_ref, high_ref, own_ref, oth_ref, *rest):
    outs, acc_ref = rest[:NX], rest[NX]
    colour = pl.program_id(1)
    n_moms = cos_ref.shape[0]
    count = high_ref.shape[-1]
    step = 512
    total = None
    for j in range(0, count, step):
        cut = pl.ds(j, step)
        real = high_ref[0, 0, 0, :, cut].astype(jnp.float32)
        imag = high_ref[0, 1, 0, :, cut].astype(jnp.float32)
        reals, imags = [], []
        for p in range(n_moms):
            cosine = jnp.concatenate([cos_ref[p, :, cut]] * 2, 0)
            sine = jnp.concatenate([sin_ref[p, :, cut]] * 2, 0)
            reals.append((real * cosine - imag * sine).astype(jnp.bfloat16))
            imags.append((real * sine + imag * cosine).astype(jnp.bfloat16))
        phased = jnp.concatenate(reals + imags, 0)
        low = jnp.concatenate([own_ref[0, 0, :, cut], oth_ref[0, 0, :, cut]], 0)
        part = lax.dot_general(
            low, phased, (((1,), (1,)), ((), ())), preferred_element_type=jnp.float32
        )
        total = part if total is None else total + part

    @pl.when(colour == 0)
    def _():
        acc_ref[...] = total

    @pl.when(colour > 0)
    def _():
        acc_ref[...] += total

    @pl.when(colour == pl.num_programs(1) - 1)
    def _():
        x, _, _ = coords()
        half = 128
        pattern = pat_ref[0:1, :]
        is_spin = [jnp.broadcast_to(pattern == a, (16, half)) for a in range(4)]
        low_pair = pattern < 2
        odd = jnp.logical_or(pattern == 1, pattern == 3)
        mesons = [[], [], [], []]
        for owner in range(2):
            over = []
            for s in range(4):
                u0 = owner * 128 + s * 16
                u1 = u0 + 64
                over.append(
                    (
                        acc_ref[u0 : u0 + 16, :half] + acc_ref[u1 : u1 + 16, half:],
                        acc_ref[u1 : u1 + 16, :half] - acc_ref[u0 : u0 + 16, half:],
                    )
                )
            for g in range(4):
                picked = []
                for u in range(2):
                    value = over[PARTNER[g][3]][u]
                    for a in range(3):
                        value = jnp.where(is_spin[a], over[PARTNER[g][a]][u], value)
                    picked.append(value)
                re, im = picked
                if g == 2:
                    re, im = jnp.where(low_pair, -im, im), jnp.where(low_pair, re, -re)
                if g == 3:
                    re, im = jnp.where(odd, re, -re), jnp.where(odd, im, -im)
                mesons[g] += [re, im]
        stacked = [jnp.concatenate(m, 0) for m in mesons]
        lane = lax.broadcasted_iota(jnp.int32, stacked[0].shape, 1) // 32
        for k in range(NX):
            group = lax.rem(x + k, NX)
            result = None
            for g in range(4):
                turned = pltpu.roll(stacked[g], lax.rem(g - group + NX, NX) * 32, 1)
                result = turned if result is None else jnp.where(lane == g, turned, result)
            outs[k][0] = result


def contract(pattern_lanes, cosines, sines, high, low_own, low_oth, first, number):
    colours, rows, count = low_own.shape[1:]
    offset = first if high.shape[0] == SLOTS else 0
    whole = lambda shape: pl.BlockSpec(shape, lambda i, c: (0,) * len(shape))
    low_spec = pl.BlockSpec((1, 1, rows, count), lambda i, c: (first + i, c, 0, 0))
    flops = 2 * number * colours * 256 * 256 * count
    return pl.pallas_call(
        contract_body,
        grid=(number, colours),
        in_specs=[
            whole(pattern_lanes.shape),
            whole(cosines.shape),
            whole(sines.shape),
            pl.BlockSpec((1, 2, 1, 16, count), lambda i, c: (offset + i, 0, c, 0, 0)),
            low_spec,
            low_spec,
        ],
        out_specs=[pl.BlockSpec((1, 64, 128), lambda i, c: (i, 0, 0))] * NX,
        out_shape=[jax.ShapeDtypeStruct((number, 64, 128), jnp.float32)] * NX,
        scratch_shapes=[pltpu.VMEM((256, 256), jnp.float32)],
        compiler_params=pltpu.CompilerParams(vmem_limit_bytes=20 * 2**20),
        cost_estimate=pl.CostEstimate(
            flops=flops, bytes_accessed=number * colours * rows * count * 4, transcendentals=0
        ),
        name="contract",
    )(pattern_lanes, cosines, sines, high, low_own, low_oth)


def assemble_body(a_ref, b_ref, c_ref, d_ref, out_ref):
    mode = lax.axis_index("mode")
    blocks = [mode, mode ^ 2, mode ^ 1, mode ^ 3]
    lane = lax.broadcasted_iota(jnp.int32, (32, 128), 1) // 16
    held = [a_ref[...], b_ref[...], c_ref[...], d_ref[...]]
    for g in range(4):
        for p in range(2):
            result = None
            for ref, block in zip(held, blocks):
                shift = lax.rem(block * 16 - (g * 32 + p * 16) + 128, 128)
                turned = pltpu.roll(ref, shift, 1)
                result = turned if result is None else jnp.where(lane == block, turned, result)
            for u in range(2):
                out_ref[g, u, p] = result[u * 16 : u * 16 + 16, :64]


def assemble(pieces):
    return pl.pallas_call(
        assemble_body,
        out_shape=jax.ShapeDtypeStruct((4, 2, 2, 16, 64), jnp.float32),
        name="assemble",
    )(*pieces)


def phase_tables(momenta, first_site, count):
    sites = first_site + jnp.arange(count, dtype=jnp.int32)
    coords = jnp.stack([sites % 32, sites // 32 % 32, sites // 1024])
    turns = jnp.sum(momenta[:, :, None] * coords[None, :, :], axis=1)
    angles = turns.astype(jnp.float32) * (2.0 * math.pi / 96.0)
    wide = lambda a: jnp.broadcast_to(a[:, None, :], (a.shape[0], 8, count))
    return wide(jnp.cos(angles)), wide(jnp.sin(angles))


def sum_x(parts):
    moved = [move(parts[k], 0, 0, k) for k in (1, 2, 3)]
    return parts[0] + moved[0] + moved[1] + moved[2]


def sum_y(slots):
    moved = [move(slots[:, k - 1], k, 0, 0) for k in (1, 2, 3)]
    total = moved[0] + moved[1] + moved[2]
    return total + slots[:, 3] if slots.shape[1] == NY else total


def body(low_modes, high_modes, pattern, momenta):
    count = low_modes.shape[-1]
    my_mode = lax.axis_index("mode")
    high = relayout_high(high_modes)
    chunks = ((0, 4), (4, 3), (7, 1))
    arrived = [flip(high[first : first + number], 2) for first, number in chunks]

    low_own = relayout_low(low_modes)
    low_own = low_own.reshape(low_own.shape[0], low_own.shape[1], -1, count)
    low_oth = flip(low_own, 1)
    cosines, sines = phase_tables(momenta, lax.axis_index("site") * count, count)

    def lanes(block):
        part = lax.dynamic_slice_in_dim(pattern, block * 16, 16, 0)
        return jnp.broadcast_to(jnp.tile(part, 8)[None, :], (8, 128))

    own = contract(lanes(my_mode), cosines, sines, high, low_own, low_oth, 0, SLOTS)
    lanes_recv = lanes(my_mode ^ 2)
    recv = [
        contract(lanes_recv, cosines, sines, block, low_own, low_oth, first, number)
        for block, (first, number) in zip(arrived, chunks)
    ]
    own_x = sum_x(own)
    own_y = sum_y(own_x.reshape(2, NY, 64, 128))
    first_y = sum_y(sum_x(recv[0])[None])
    across = move(jnp.concatenate([own_y[:1], first_y]), 0, 1, 0)
    second_y = sum_y(sum_x(recv[1])[None])
    last = sum_x(recv[2])
    total = jnp.concatenate([own_y[1:], second_y + last]) + across
    other = flip(total[:, 32:], 1)
    pieces = (total[0, :32], total[1, :32], other[0], other[1])
    return jnp.transpose(assemble(pieces), (0, 1, 2, 4, 3))


def solution(mesh):
    placed = (
        P("mode", None, None, None, None, "site"),
        P("mode", None, None, None, "site"),
        P(),
        P(),
    )
    return jax.shard_map(
        body,
        mesh=mesh,
        in_specs=placed,
        out_specs=P(None, None, "site", None, "mode"),
        check_vma=False,
    )
```

```python
import functools
import math

import jax
import jax.numpy as jnp
from jax import lax
from jax.experimental import pallas as pl
from jax.experimental.pallas import tpu as pltpu
from jax.sharding import PartitionSpec as P

NX, NY, NZ = 4, 4, 2
SLOTS = NY * NZ
PARTNER = ((0, 1, 2, 3), (2, 3, 0, 1), (3, 2, 1, 0), (1, 0, 3, 2))
OWNERS = (2, 1, 3, 0)


def coords():
    site = lax.axis_index("site")
    return lax.rem(site, 4), lax.div(site, 8), lax.rem(lax.div(site, 4), 2)


def site_of(y, z, x):
    return ((y % NY) * NZ + z % NZ) * NX + x % NX


def trade(block, ymask, zmask, xmask):
    route = [
        (site_of(y, z, x), site_of(y ^ ymask, z ^ zmask, x ^ xmask))
        for y in range(NY)
        for z in range(NZ)
        for x in range(NX)
    ]
    return lax.ppermute(block, "site", route)


def flip(block, mask):
    return lax.ppermute(block, "mode", [(i, i ^ mask) for i in range(4)])


def slot_of(t, y, z):
    far = (t // 2) ^ y
    place = jnp.where(far == 2, 0, jnp.where(far == 1, 1, jnp.where(far == 3, 2, 3)))
    return jnp.where(t % 2 == z, NY, 0) + place


def time_of(slot, y, z):
    plane = z if slot >= NY else 1 - z
    return 2 * (y ^ OWNERS[slot % NY]) + plane


VMEM = pl.BlockSpec(memory_space=pltpu.VMEM)
STEP = 512
HIGH_LIMIT = 4 * 2**20
LOW_LIMIT = 10 * 2**20
SMALL = pltpu.CompilerParams(vmem_limit_bytes=4 * 2**20)
TOKEN = jax.ShapeDtypeStruct((8, 128), jnp.float32)
TINY = pl.CostEstimate(flops=0, bytes_accessed=0, transcendentals=0)


def whole(shape):
    return pl.BlockSpec(shape, lambda *_: (0,) * len(shape))


def relayout_high_body(in_ref, *refs):
    outs, token_ref, turned_ref = refs[:-2], refs[-2], refs[-1]
    _, y, z = coords()
    token_ref[...] = jnp.zeros_like(token_ref)

    def one(index, carry):
        r, c = lax.div(index, 3), lax.rem(index, 3)
        for j in range(0, in_ref.shape[-1], STEP):
            cut = pl.ds(j, STEP)
            values = in_ref[:, r, c, :, cut].astype(jnp.float32)
            turned_ref[...] = jnp.swapaxes(values, 0, 1).astype(jnp.bfloat16)
            slot = 0
            for out in outs:
                for k in range(out.shape[0]):
                    out[k, r, c, :, cut] = turned_ref[time_of(slot, y, z)]
                    slot += 1
        return carry

    lax.fori_loop(0, 6, one, 0)


def relayout_high(high, sizes):
    rows, two, colours, slices, count = high.shape
    return pl.pallas_call(
        relayout_high_body,
        in_specs=[VMEM],
        out_specs=[VMEM] * (len(sizes) + 1),
        out_shape=[
            jax.ShapeDtypeStruct((n, two, colours, rows, count), jnp.bfloat16) for n in sizes
        ]
        + [jax.ShapeDtypeStruct((8, 128), jnp.float32)],
        scratch_shapes=[pltpu.VMEM((slices, rows, STEP), jnp.bfloat16)],
        compiler_params=pltpu.CompilerParams(vmem_limit_bytes=HIGH_LIMIT),
        cost_estimate=TINY,
        name="relayout_high",
    )(high)


def relayout_low_body(in_ref, after_ref, out_ref, token_ref):
    token_ref[...] = jnp.zeros_like(token_ref)
    _, y, z = coords()

    def one(s, carry):
        for j in range(0, in_ref.shape[-1], STEP):
            cut = pl.ds(j, STEP)
            values = in_ref[:, s, 0, 0, :, cut].astype(jnp.float32)
            turned = jnp.swapaxes(values, 0, 1).astype(jnp.bfloat16)
            for t in range(SLOTS):
                out_ref[slot_of(t, y, z), 0, 0, s, :, cut] = turned[t]
        return carry

    lax.fori_loop(0, in_ref.shape[1], one, 0)


def relayout_low(low, token):
    rows, spins, two, colours, slices, count = low.shape
    turned, token = pl.pallas_call(
        relayout_low_body,
        grid=(colours, two),
        in_specs=[
            pl.BlockSpec((rows, spins, 1, 1, slices, count), lambda c, u: (0, 0, u, c, 0, 0)),
            whole((8, 128)),
        ],
        out_specs=[
            pl.BlockSpec((slices, 1, 1, spins, rows, count), lambda c, u: (0, c, u, 0, 0, 0)),
            whole((8, 128)),
        ],
        out_shape=[
            jax.ShapeDtypeStruct((slices, colours, two, spins, rows, count), jnp.bfloat16),
            jax.ShapeDtypeStruct((8, 128), jnp.float32),
        ],
        compiler_params=pltpu.CompilerParams(vmem_limit_bytes=LOW_LIMIT),
        cost_estimate=TINY,
        name="relayout_low",
    )(low, token)
    return turned.reshape(slices, colours, two * spins * rows, count), token


def contract_body(by_part, added, pat_ref, cos_ref, sin_ref, own_ref, oth_ref, *refs):
    highs, adds, outs = refs[:2], refs[2 : 2 + added], refs[3 + added : -2]
    token_ref, acc_ref = refs[-2:]
    token_ref[...] = jnp.zeros_like(token_ref)
    n_moms, count = cos_ref.shape
    x, _, _ = coords()
    acc_ref[...] = jnp.zeros_like(acc_ref)

    def one(colour, carry):
        total = None
        for j in range(0, count, STEP):
            cut = pl.ds(j, STEP)
            rows = []
            for high_ref in highs:
                real = high_ref[0, 0, colour, :, cut].astype(jnp.float32)
                imag = high_ref[0, 1, colour, :, cut].astype(jnp.float32)
                reals, imags = [], []
                for p in range(n_moms):
                    cosine = cos_ref[p : p + 1, cut]
                    sine = sin_ref[p : p + 1, cut]
                    reals.append((real * cosine - imag * sine).astype(jnp.bfloat16))
                    imags.append((real * sine + imag * cosine).astype(jnp.bfloat16))
                rows += reals + imags
            phased = jnp.concatenate(rows, 0)
            low = jnp.concatenate([own_ref[0, colour, :, cut], oth_ref[0, colour, :, cut]], 0)
            part = lax.dot_general(
                low, phased, (((1,), (1,)), ((), ())), preferred_element_type=jnp.float32
            )
            total = part if total is None else total + part
        acc_ref[...] += total
        return carry

    lax.fori_loop(0, 3, one, 0)
    half = 128
    for block in range(2):
        base = block * 256
        pattern = pat_ref[0:1, block * half : block * half + half]
        is_spin = [jnp.broadcast_to(pattern == a, (16, half)) for a in range(4)]
        low_pair = pattern < 2
        odd = jnp.logical_or(pattern == 1, pattern == 3)
        mesons = [[], [], [], []]
        for owner in range(2):
            over = []
            for s in range(4):
                u0 = slice(owner * 128 + s * 16, owner * 128 + s * 16 + 16)
                u1 = slice(owner * 128 + s * 16 + 64, owner * 128 + s * 16 + 80)
                r0, r1 = slice(base, base + half), slice(base + half, base + 2 * half)
                over.append((acc_ref[u0, r0] + acc_ref[u1, r1], acc_ref[u1, r0] - acc_ref[u0, r1]))
            for g in range(4):
                picked = []
                for u in range(2):
                    value = over[PARTNER[g][3]][u]
                    for a in range(3):
                        value = jnp.where(is_spin[a], over[PARTNER[g][a]][u], value)
                    picked.append(value)
                re, im = picked
                if g == 2:
                    re, im = jnp.where(low_pair, -im, im), jnp.where(low_pair, re, -re)
                if g == 3:
                    re, im = jnp.where(odd, re, -re), jnp.where(odd, im, -im)
                mesons[g] += [re, im]
        stacked = [jnp.concatenate(m, 0) for m in mesons]
        lane = lax.broadcasted_iota(jnp.int32, stacked[0].shape, 1) // 32
        for k in range(NX):
            group = x ^ OWNERS[k]
            result = None
            for g in range(4):
                turned = pltpu.roll(stacked[g], lax.rem(g - group + NX, NX) * 32, 1)
                result = turned if result is None else jnp.where(lane == g, turned, result)
            for add in adds:
                result = result + add[k, block].astype(jnp.float32)
            if by_part:
                outs[k // 2][k % 2, 0, block] = result.astype(outs[k // 2].dtype)
            else:
                outs[0][0, k, block] = result.astype(outs[0].dtype)


def contract(tables, low_own, low_oth, own, received, first, by_part, sent, after, adds=()):
    colours, rows, count = low_own.shape[1:]
    number = own.shape[0]
    unit = (2, 64, 128)
    if by_part:
        shapes = [
            jax.ShapeDtypeStruct((2, number) + unit, sent),
            jax.ShapeDtypeStruct((2, number) + unit, jnp.float32),
        ]
        out_specs = [pl.BlockSpec((2, 1) + unit, lambda i: (0, i, 0, 0, 0))] * 2
    else:
        shapes = [jax.ShapeDtypeStruct((number, NX) + unit, sent)]
        out_specs = [pl.BlockSpec((1, NX) + unit, lambda i: (i, 0, 0, 0, 0))]
    high_spec = pl.BlockSpec((1, 2, colours, 16, count), lambda i: (i, 0, 0, 0, 0))
    low_spec = pl.BlockSpec((1, colours, rows, count), lambda i: (first + i, 0, 0, 0))
    return pl.pallas_call(
        functools.partial(contract_body, by_part, len(adds)),
        grid=(number,),
        in_specs=[whole(t.shape) for t in tables]
        + [low_spec, low_spec, high_spec, high_spec]
        + [whole(a.shape) for a in adds]
        + [whole((8, 128))],
        out_specs=out_specs + [whole((8, 128))],
        out_shape=shapes + [TOKEN],
        scratch_shapes=[pltpu.VMEM((256, 512), jnp.float32)],
        compiler_params=pltpu.CompilerParams(vmem_limit_bytes=14 * 2**20),
        cost_estimate=TINY,
        name=f"contract_{first}_{number}",
    )(*tables, low_own, low_oth, own, received, *adds, after)


def fold_body(axis, kept_ref, got_ref, after_ref, first_ref, second_ref, token_ref):
    half = kept_ref.shape[axis] // 2
    for out_ref, cut in ((first_ref, slice(0, half)), (second_ref, slice(half, 2 * half))):
        index = (slice(None),) * axis + (cut,)
        total = kept_ref[index] + got_ref[index].astype(jnp.float32)
        out_ref[...] = total.astype(out_ref.dtype)
    token_ref[...] = jnp.zeros_like(token_ref)


def fold(kept, got, axis, sent, after):
    shape = kept.shape[:axis] + (kept.shape[axis] // 2,) + kept.shape[axis + 1 :]
    return pl.pallas_call(
        functools.partial(fold_body, axis),
        in_specs=[VMEM] * 3,
        out_specs=[VMEM] * 3,
        out_shape=[
            jax.ShapeDtypeStruct(shape, sent),
            jax.ShapeDtypeStruct(shape, jnp.float32),
            TOKEN,
        ],
        compiler_params=SMALL,
        cost_estimate=TINY,
        name="fold",
    )(kept, got, after)


def finish_body(kept_ref, last_ref, across_ref, mine_ref, other_ref):
    for out_ref, rows in ((mine_ref, slice(0, 32)), (other_ref, slice(32, 64))):
        out_ref[...] = kept_ref[0, :, rows] + last_ref[0, :, rows] + across_ref[0, :, rows]


def finish(kept, last, across):
    return pl.pallas_call(
        finish_body,
        in_specs=[VMEM] * 3,
        out_specs=[VMEM] * 2,
        out_shape=[jax.ShapeDtypeStruct((2, 32, 128), jnp.float32)] * 2,
        compiler_params=SMALL,
        cost_estimate=TINY,
        name="finish",
    )(kept, last, across)


def assemble_body(mine_ref, other_ref, out_ref):
    mode = lax.axis_index("mode")
    blocks = [mode, mode ^ 2, mode ^ 1, mode ^ 3]
    lane = lax.broadcasted_iota(jnp.int32, (32, 128), 1) // 16
    held = [mine_ref[0], mine_ref[1], other_ref[0], other_ref[1]]
    for g in range(4):
        for p in range(2):
            result = None
            for values, block in zip(held, blocks):
                shift = lax.rem(block * 16 - (g * 32 + p * 16) + 128, 128)
                turned = pltpu.roll(values, shift, 1)
                result = turned if result is None else jnp.where(lane == block, turned, result)
            for u in range(2):
                out_ref[g, u, p] = result[u * 16 : u * 16 + 16, :64]


def assemble(pieces):
    return pl.pallas_call(
        assemble_body,
        out_shape=jax.ShapeDtypeStruct((4, 2, 2, 16, 64), jnp.float32),
        compiler_params=SMALL,
        cost_estimate=TINY,
        name="assemble",
    )(*pieces)


def phase_tables(momenta, first_site, count):
    sites = first_site + jnp.arange(count, dtype=jnp.int32)
    coords = jnp.stack([sites % 32, sites // 32 % 32, sites // 1024])
    turns = jnp.sum(momenta[:, :, None] * coords[None, :, :], axis=1)
    angles = turns.astype(jnp.float32) * (2.0 * math.pi / 96.0)
    return jnp.cos(angles), jnp.sin(angles)


def body(low_modes, high_modes, pattern, momenta):
    count = low_modes.shape[-1]
    my_mode = lax.axis_index("mode")
    wide, narrow = jnp.float32, jnp.bfloat16
    *high, token = relayout_high(high_modes, (4, 2, 1, 1))
    arrived = [flip(chunk, 2) for chunk in high]

    low_oth = flip(low_modes, 1)
    low_own, token = relayout_low(low_modes, token)
    low_oth, _ = relayout_low(low_oth, token)
    cosines, sines = phase_tables(momenta, lax.axis_index("site") * count, count)

    def lanes(block):
        part = lax.dynamic_slice_in_dim(pattern, block * 16, 16, 0)
        return jnp.broadcast_to(jnp.tile(part, 8)[None, :], (8, 128))

    tables = (jnp.concatenate([lanes(my_mode), lanes(my_mode ^ 2)], 1), cosines, sines)
    away, far, token = contract(
        tables, low_own, low_oth, high[0], arrived[0], 0, True, narrow, token
    )
    far_got = trade(away, 0, 0, 1)
    away, token = contract(
        tables, low_own, low_oth, high[1], arrived[1], 4, False, narrow, token
    )
    near_got = trade(away, 1, 0, 0)
    away, far, token = fold(far, far_got, 0, narrow, token)
    far_got = trade(away, 0, 0, 3)
    near, token = contract(tables, low_own, low_oth, high[2], arrived[2], 6, False, wide, token)
    near_last = trade((near[0] + near_got[0].astype(wide)).astype(narrow), 3, 0, 0)
    away, far, token = fold(far[0], far_got[0], 0, wide, token)
    far_got = trade(away, 1, 0, 0)
    adds = (near_got[1], near_last)
    away, near, token = contract(
        tables, low_own, low_oth, high[3], arrived[3], 7, True, wide, token, adds
    )
    near_got = trade(away, 0, 0, 1)
    away, far, token = fold(far, far_got, 0, wide, token)
    far_got = trade(away, 3, 0, 0)
    away, near, token = fold(near[:, 0], near_got[:, 0], 0, wide, token)
    near_got = trade(away, 0, 0, 3)
    across = trade(far + far_got, 0, 1, 0)
    mine, other = finish(near, near_got, across)
    pieces = (mine, flip(other, 1))
    return jnp.transpose(assemble(pieces), (0, 1, 2, 4, 3))


def solution(mesh):
    placed = (
        P("mode", None, None, None, None, "site"),
        P("mode", None, None, None, "site"),
        P(),
        P(),
    )
    return jax.shard_map(
        body,
        mesh=mesh,
        in_specs=placed,
        out_specs=P(None, None, "site", None, "mode"),
        check_vma=False,
    )
```

```python
import functools
import math

import jax
import jax.numpy as jnp
from jax import lax
from jax.experimental import pallas as pl
from jax.experimental.pallas import tpu as pltpu
from jax.sharding import PartitionSpec as P

NX, NY, NZ = 4, 4, 2
SLOTS = NY * NZ
PARTNER = ((0, 1, 2, 3), (2, 3, 0, 1), (3, 2, 1, 0), (1, 0, 3, 2))
OWNERS = (2, 1, 3, 0)


def coords():
    site = lax.axis_index("site")
    return lax.rem(site, 4), lax.div(site, 8), lax.rem(lax.div(site, 4), 2)


def site_of(y, z, x):
    return ((y % NY) * NZ + z % NZ) * NX + x % NX


def trade(block, ymask, zmask, xmask):
    route = [
        (site_of(y, z, x), site_of(y ^ ymask, z ^ zmask, x ^ xmask))
        for y in range(NY)
        for z in range(NZ)
        for x in range(NX)
    ]
    return lax.ppermute(block, "site", route)


def flip(block, mask):
    return lax.ppermute(block, "mode", [(i, i ^ mask) for i in range(4)])


def slot_of(t, y, z):
    far = (t // 2) ^ y
    place = jnp.where(far == 2, 0, jnp.where(far == 1, 1, jnp.where(far == 3, 2, 3)))
    return jnp.where(t % 2 == z, NY, 0) + place


def time_of(slot, y, z):
    plane = z if slot >= NY else 1 - z
    return 2 * (y ^ OWNERS[slot % NY]) + plane


VMEM = pl.BlockSpec(memory_space=pltpu.VMEM)
STEP = 512
HIGH_LIMIT = 12 * 2**20
LOW_LIMIT = 16 * 2**20
MANY_LIMIT = 24 * 2**20
FEW_LIMIT = 14 * 2**20
SMALL = pltpu.CompilerParams(vmem_limit_bytes=4 * 2**20)
TOKEN = jax.ShapeDtypeStruct((8, 128), jnp.float32)
TINY = pl.CostEstimate(flops=0, bytes_accessed=0, transcendentals=0)


def stay(array):
    return pltpu.with_memory_space_constraint(array, pltpu.HBM)


def whole(shape):
    return pl.BlockSpec(shape, lambda *_: (0,) * len(shape))


def turn(values, turned_ref, outs, index, cut, y, z):
    turned_ref[...] = jnp.swapaxes(values, 0, 1)
    slot = 0
    for out in outs:
        for k in range(out.shape[0]):
            out[(k,) + index + (slice(None), cut)] = turned_ref[time_of(slot, y, z)]
            slot += 1


def relayout_high_body(in_ref, *refs):
    outs, (token_ref, held_ref, turned_ref, sems) = refs[:-4], refs[-4:]
    _, y, z = coords()
    token_ref[...] = jnp.zeros_like(token_ref)
    pieces = [(r, c) for r in range(2) for c in range(3)]
    copies = [
        pltpu.make_async_copy(in_ref.at[:, r, c], held_ref.at[i], sems.at[i])
        for i, (r, c) in enumerate(pieces)
    ]
    for copy in copies:
        copy.start()
    for i, (r, c) in enumerate(pieces):
        copies[i].wait()
        for j in range(0, held_ref.shape[-1], STEP):
            cut = pl.ds(j, STEP)
            turn(held_ref[i, :, :, cut], turned_ref, outs, (r, c), cut, y, z)


def relayout_high(high, sizes):
    rows, two, colours, slices, count = high.shape
    return pl.pallas_call(
        relayout_high_body,
        in_specs=[pl.BlockSpec(memory_space=pl.ANY)],
        out_specs=[VMEM] * (len(sizes) + 1),
        out_shape=[pltpu.VMEM((n, two, colours, rows, count), jnp.bfloat16) for n in sizes]
        + [TOKEN],
        scratch_shapes=[
            pltpu.VMEM((two * colours, rows, slices, count), jnp.bfloat16),
            pltpu.VMEM((slices, rows, STEP), jnp.bfloat16),
            pltpu.SemaphoreType.DMA((two * colours,)),
        ],
        compiler_params=pltpu.CompilerParams(vmem_limit_bytes=HIGH_LIMIT),
        cost_estimate=TINY,
        name="relayout_high",
    )(stay(high))


def relayout_low_body(in_ref, after_ref, many_ref, few_ref, token_ref, turned_ref):
    _, y, z = coords()
    token_ref[...] = jnp.zeros_like(token_ref)

    def one(s, carry):
        for j in range(0, in_ref.shape[-1], STEP):
            cut = pl.ds(j, STEP)
            values = in_ref[:, s, 0, 0, :, cut]
            turn(values, turned_ref, (many_ref, few_ref), (0, 0, s), cut, y, z)
        return carry

    lax.fori_loop(0, in_ref.shape[1], one, 0)


def relayout_low(low, after, sizes):
    rows, spins, two, colours, slices, count = low.shape
    *turned, token = pl.pallas_call(
        relayout_low_body,
        grid=(colours, two),
        in_specs=[
            pl.BlockSpec((rows, spins, 1, 1, slices, count), lambda c, u: (0, 0, u, c, 0, 0)),
            whole((8, 128)),
        ],
        out_specs=[
            pl.BlockSpec((n, 1, 1, spins, rows, count), lambda c, u: (0, c, u, 0, 0, 0))
            for n in sizes
        ]
        + [whole((8, 128))],
        out_shape=[
            space((n, colours, two, spins, rows, count), jnp.bfloat16)
            for n, space in zip(sizes, (pltpu.HBM, pltpu.VMEM))
        ]
        + [TOKEN],
        scratch_shapes=[pltpu.VMEM((slices, rows, STEP), jnp.bfloat16)],
        compiler_params=pltpu.CompilerParams(vmem_limit_bytes=LOW_LIMIT),
        cost_estimate=TINY,
        name="relayout_low",
    )(stay(low), after)
    turned = [t.reshape(t.shape[0], colours, two * spins * rows, count) for t in turned]
    return turned, token


def contract_body(by_part, added, pat_ref, cos_ref, sin_ref, own_ref, oth_ref, *refs):
    highs, adds, outs = refs[:2], refs[2 : 2 + added], refs[3 + added : -2]
    token_ref, acc_ref = refs[-2:]
    token_ref[...] = jnp.zeros_like(token_ref)
    n_moms, count = cos_ref.shape
    x, _, _ = coords()
    acc_ref[...] = jnp.zeros_like(acc_ref)

    def one(colour, carry):
        total = None
        for j in range(0, count, STEP):
            cut = pl.ds(j, STEP)
            rows = []
            for high_ref in highs:
                real = high_ref[0, 0, colour, :, cut].astype(jnp.float32)
                imag = high_ref[0, 1, colour, :, cut].astype(jnp.float32)
                reals, imags = [], []
                for p in range(n_moms):
                    cosine = cos_ref[p : p + 1, cut]
                    sine = sin_ref[p : p + 1, cut]
                    reals.append((real * cosine - imag * sine).astype(jnp.bfloat16))
                    imags.append((real * sine + imag * cosine).astype(jnp.bfloat16))
                rows += reals + imags
            phased = jnp.concatenate(rows, 0)
            low = jnp.concatenate([own_ref[0, colour, :, cut], oth_ref[0, colour, :, cut]], 0)
            part = lax.dot_general(
                low, phased, (((1,), (1,)), ((), ())), preferred_element_type=jnp.float32
            )
            total = part if total is None else total + part
        acc_ref[...] += total
        return carry

    lax.fori_loop(0, 3, one, 0)
    half = 128
    for block in range(2):
        base = block * 256
        pattern = pat_ref[0:1, block * half : block * half + half]
        is_spin = [jnp.broadcast_to(pattern == a, (16, half)) for a in range(4)]
        low_pair = pattern < 2
        odd = jnp.logical_or(pattern == 1, pattern == 3)
        mesons = [[], [], [], []]
        for owner in range(2):
            over = []
            for s in range(4):
                u0 = slice(owner * 128 + s * 16, owner * 128 + s * 16 + 16)
                u1 = slice(owner * 128 + s * 16 + 64, owner * 128 + s * 16 + 80)
                r0, r1 = slice(base, base + half), slice(base + half, base + 2 * half)
                over.append((acc_ref[u0, r0] + acc_ref[u1, r1], acc_ref[u1, r0] - acc_ref[u0, r1]))
            for g in range(4):
                picked = []
                for u in range(2):
                    value = over[PARTNER[g][3]][u]
                    for a in range(3):
                        value = jnp.where(is_spin[a], over[PARTNER[g][a]][u], value)
                    picked.append(value)
                re, im = picked
                if g == 2:
                    re, im = jnp.where(low_pair, -im, im), jnp.where(low_pair, re, -re)
                if g == 3:
                    re, im = jnp.where(odd, re, -re), jnp.where(odd, im, -im)
                mesons[g] += [re, im]
        stacked = [jnp.concatenate(m, 0) for m in mesons]
        lane = lax.broadcasted_iota(jnp.int32, stacked[0].shape, 1) // 32
        for k in range(NX):
            group = x ^ OWNERS[k]
            result = None
            for g in range(4):
                turned = pltpu.roll(stacked[g], lax.rem(g - group + NX, NX) * 32, 1)
                result = turned if result is None else jnp.where(lane == g, turned, result)
            for add in adds:
                result = result + add[add.shape[0] - 1, k, block].astype(jnp.float32)
            if by_part == "each":
                outs[k][0, block] = result.astype(outs[k].dtype)
            elif by_part:
                outs[k // 2][k % 2, 0, block] = result.astype(outs[k // 2].dtype)
            else:
                outs[0][0, k, block] = result.astype(outs[0].dtype)


def contract(tables, lows, own, received, first, by_part, sent, after, limit, adds=()):
    colours, rows, count = lows[0].shape[1:]
    number = own.shape[0]
    unit = (2, 64, 128)
    if by_part == "each":
        kinds = [sent] * (NX - 1) + [jnp.float32]
        shapes = [jax.ShapeDtypeStruct((number,) + unit, kind) for kind in kinds]
        out_specs = [pl.BlockSpec((1,) + unit, lambda i: (i, 0, 0, 0))] * NX
    elif by_part:
        shapes = [
            jax.ShapeDtypeStruct((2, number) + unit, sent),
            jax.ShapeDtypeStruct((2, number) + unit, jnp.float32),
        ]
        out_specs = [pl.BlockSpec((2, 1) + unit, lambda i: (0, i, 0, 0, 0))] * 2
    else:
        shapes = [jax.ShapeDtypeStruct((number, NX) + unit, sent)]
        out_specs = [pl.BlockSpec((1, NX) + unit, lambda i: (i, 0, 0, 0, 0))]
    high_spec = pl.BlockSpec((1, 2, colours, 16, count), lambda i: (i, 0, 0, 0, 0))
    low_spec = pl.BlockSpec((1, colours, rows, count), lambda i: (first + i, 0, 0, 0))
    return pl.pallas_call(
        functools.partial(contract_body, by_part, len(adds)),
        grid=(number,),
        in_specs=[whole(t.shape) for t in tables]
        + [low_spec, low_spec, high_spec, high_spec]
        + [whole(a.shape) for a in adds]
        + [whole((8, 128))],
        out_specs=out_specs + [whole((8, 128))],
        out_shape=shapes + [TOKEN],
        scratch_shapes=[pltpu.VMEM((256, 512), jnp.float32)],
        compiler_params=pltpu.CompilerParams(vmem_limit_bytes=limit),
        cost_estimate=TINY,
        name=f"contract_{first}_{number}",
    )(*tables, *lows, own, received, *adds, after)


def fold_body(number, *refs):
    parts, (first_ref, second_ref, token_ref) = refs[:number], refs[-3:]
    half = parts[0].shape[0] // 2
    for out_ref, cut in ((first_ref, slice(0, half)), (second_ref, slice(half, 2 * half))):
        total = None
        for part in parts:
            value = part[cut].astype(jnp.float32)
            total = value if total is None else total + value
        out_ref[...] = total.astype(out_ref.dtype)
    token_ref[...] = jnp.zeros_like(token_ref)


def fold(parts, sent, after):
    shape = (parts[0].shape[0] // 2,) + parts[0].shape[1:]
    return pl.pallas_call(
        functools.partial(fold_body, len(parts)),
        in_specs=[VMEM] * (len(parts) + 1),
        out_specs=[VMEM] * 3,
        out_shape=[
            jax.ShapeDtypeStruct(shape, sent),
            jax.ShapeDtypeStruct(shape, jnp.float32),
            TOKEN,
        ],
        compiler_params=SMALL,
        cost_estimate=TINY,
        name="fold",
    )(*parts, after)


def plus_body(number, *refs):
    parts, out_ref, token_ref = refs[:number], refs[-2], refs[-1]
    total = None
    for part in parts:
        value = part[: out_ref.shape[0]].astype(jnp.float32)
        total = value if total is None else total + value
    out_ref[...] = total.astype(out_ref.dtype)
    token_ref[...] = jnp.zeros_like(token_ref)


def plus(parts, sent, after):
    length = min(part.shape[0] for part in parts)
    return pl.pallas_call(
        functools.partial(plus_body, len(parts)),
        in_specs=[VMEM] * (len(parts) + 1),
        out_specs=[VMEM] * 2,
        out_shape=[jax.ShapeDtypeStruct((length,) + parts[0].shape[1:], sent), TOKEN],
        compiler_params=SMALL,
        cost_estimate=TINY,
        name="plus",
    )(*parts, after)


def finish_body(kept_ref, last_ref, across_ref, mine_ref, other_ref):
    for out_ref, rows in ((mine_ref, slice(0, 32)), (other_ref, slice(32, 64))):
        out_ref[...] = kept_ref[0, :, rows] + last_ref[0, :, rows].astype(jnp.float32) + across_ref[0, :, rows]


def finish(kept, last, across):
    return pl.pallas_call(
        finish_body,
        in_specs=[VMEM] * 3,
        out_specs=[VMEM] * 2,
        out_shape=[jax.ShapeDtypeStruct((2, 32, 128), jnp.float32)] * 2,
        compiler_params=SMALL,
        cost_estimate=TINY,
        name="finish",
    )(kept, last, across)


def assemble_body(mine_ref, other_ref, out_ref):
    mode = lax.axis_index("mode")
    blocks = [mode, mode ^ 2, mode ^ 1, mode ^ 3]
    lane = lax.broadcasted_iota(jnp.int32, (32, 128), 1) // 16
    held = [mine_ref[0], mine_ref[1], other_ref[0], other_ref[1]]
    for g in range(4):
        for p in range(2):
            result = None
            for values, block in zip(held, blocks):
                shift = lax.rem(block * 16 - (g * 32 + p * 16) + 128, 128)
                turned = pltpu.roll(values, shift, 1)
                result = turned if result is None else jnp.where(lane == block, turned, result)
            for u in range(2):
                out_ref[g, u, p] = result[u * 16 : u * 16 + 16, :64]


def assemble(pieces):
    return pl.pallas_call(
        assemble_body,
        out_shape=jax.ShapeDtypeStruct((4, 2, 2, 16, 64), jnp.float32),
        compiler_params=SMALL,
        cost_estimate=TINY,
        name="assemble",
    )(*pieces)


def phase_tables(momenta, first_site, count):
    sites = first_site + jnp.arange(count, dtype=jnp.int32)
    coords = jnp.stack([sites % 32, sites // 32 % 32, sites // 1024])
    turns = jnp.sum(momenta[:, :, None] * coords[None, :, :], axis=1)
    angles = turns.astype(jnp.float32) * (2.0 * math.pi / 96.0)
    return jnp.cos(angles), jnp.sin(angles)


def body(low_modes, high_modes, pattern, momenta):
    count = low_modes.shape[-1]
    my_mode = lax.axis_index("mode")
    wide, narrow = jnp.float32, jnp.bfloat16
    *high, token = relayout_high(high_modes, (2, 2, 2, 1, 1))
    arrived = [flip(chunk, 2) for chunk in high]
    low_oth = flip(low_modes, 1)
    low_own, token = relayout_low(low_modes, token, (4, 4))
    low_oth, token = relayout_low(low_oth, token, (4, 4))
    many, few = zip(low_own, low_oth)
    many = [stay(a) for a in many]
    cosines, sines = phase_tables(momenta, lax.axis_index("site") * count, count)

    def lanes(block):
        part = lax.dynamic_slice_in_dim(pattern, block * 16, 16, 0)
        return jnp.broadcast_to(jnp.tile(part, 8)[None, :], (8, 128))

    tables = (jnp.concatenate([lanes(my_mode), lanes(my_mode ^ 2)], 1), cosines, sines)
    away, token = contract(
        tables, many, high[0], arrived[0], 0, False, narrow, token, MANY_LIMIT
    )
    far_got = trade(away, 1, 0, 0)
    far, token = contract(
        tables, many, high[1], arrived[1], 2, False, wide, token, MANY_LIMIT
    )
    away, far, token = fold((far, far_got), narrow, token)
    far_got = trade(away, 3, 0, 0)
    away, far, token = fold((far[0], far_got[0]), narrow, token)
    far_got = trade(away, 0, 0, 1)
    away, token = contract(
        tables, few, high[2], arrived[2], 0, False, narrow, token, FEW_LIMIT
    )
    near_got = trade(away, 1, 0, 0)
    near, token = contract(
        tables, few, high[3], arrived[3], 2, False, wide, token, FEW_LIMIT
    )
    away, far, token = fold((far, far_got), narrow, token)
    far_got = trade(away, 0, 0, 3)
    away, token = plus((near, near_got), narrow, token)
    adds = (near_got, trade(away, 3, 0, 0))
    away, token = plus((far, far_got), wide, token)
    across = trade(away, 0, 1, 0)
    away, near, token = contract(
        tables, few, high[4], arrived[4], 3, True, narrow, token, FEW_LIMIT, adds
    )
    last_got = trade(away, 0, 0, 1)
    away, near, token = fold((near[:, 0], last_got[:, 0]), narrow, token)
    last_got = trade(away, 0, 0, 3)
    mine, other = finish(near, last_got, across)
    pieces = (mine, flip(other, 1))
    return jnp.transpose(assemble(pieces), (0, 1, 2, 4, 3))


def solution(mesh):
    placed = (
        P("mode", None, None, None, None, "site"),
        P("mode", None, None, None, "site"),
        P(),
        P(),
    )
    return jax.shard_map(
        body,
        mesh=mesh,
        in_specs=placed,
        out_specs=P(None, None, "site", None, "mode"),
        check_vma=False,
    )
```

```python
import functools
import math

import jax
import jax.numpy as jnp
from jax import lax
from jax.experimental import pallas as pl
from jax.experimental.pallas import tpu as pltpu
from jax.sharding import PartitionSpec as P

NX, NY, NZ = 4, 4, 2
SLOTS = NY * NZ
PARTNER = ((0, 1, 2, 3), (2, 3, 0, 1), (3, 2, 1, 0), (1, 0, 3, 2))
OWNERS = (2, 1, 3, 0)


def coords():
    site = lax.axis_index("site")
    return lax.rem(site, 4), lax.div(site, 8), lax.rem(lax.div(site, 4), 2)


def site_of(y, z, x):
    return ((y % NY) * NZ + z % NZ) * NX + x % NX


def trade(block, ymask, zmask, xmask):
    route = [
        (site_of(y, z, x), site_of(y ^ ymask, z ^ zmask, x ^ xmask))
        for y in range(NY)
        for z in range(NZ)
        for x in range(NX)
    ]
    return lax.ppermute(block, "site", route)


def flip(block, mask):
    return lax.ppermute(block, "mode", [(i, i ^ mask) for i in range(4)])


def slot_of(t, y, z):
    far = (t // 2) ^ y
    place = jnp.where(far == 2, 0, jnp.where(far == 1, 1, jnp.where(far == 3, 2, 3)))
    return jnp.where(t % 2 == z, NY, 0) + place


def time_of(slot, y, z):
    plane = z if slot >= NY else 1 - z
    return 2 * (y ^ OWNERS[slot % NY]) + plane


VMEM = pl.BlockSpec(memory_space=pltpu.VMEM)
STEP = 512
HIGH_LIMIT = 12 * 2**20
LOW_LIMIT = 16 * 2**20
MANY_LIMIT = 24 * 2**20
FEW_LIMIT = 14 * 2**20
SMALL = pltpu.CompilerParams(vmem_limit_bytes=4 * 2**20)
TOKEN = jax.ShapeDtypeStruct((8, 128), jnp.float32)
TINY = pl.CostEstimate(flops=0, bytes_accessed=0, transcendentals=0)


def stay(array):
    return pltpu.with_memory_space_constraint(array, pltpu.HBM)


def whole(shape):
    return pl.BlockSpec(shape, lambda *_: (0,) * len(shape))


def turn(values, turned_ref, outs, index, cut, y, z):
    turned_ref[...] = jnp.swapaxes(values, 0, 1)
    slot = 0
    for out in outs:
        for k in range(out.shape[0]):
            out[(k,) + index + (slice(None), cut)] = turned_ref[time_of(slot, y, z)]
            slot += 1


def relayout_high_body(in_ref, *refs):
    outs, (token_ref, held_ref, turned_ref, sems) = refs[:-4], refs[-4:]
    _, y, z = coords()
    token_ref[...] = jnp.zeros_like(token_ref)
    pieces = [(r, c) for r in range(2) for c in range(3)]
    copies = [
        pltpu.make_async_copy(in_ref.at[:, r, c], held_ref.at[i], sems.at[i])
        for i, (r, c) in enumerate(pieces)
    ]
    for copy in copies:
        copy.start()
    for i, (r, c) in enumerate(pieces):
        copies[i].wait()
        for j in range(0, held_ref.shape[-1], STEP):
            cut = pl.ds(j, STEP)
            turn(held_ref[i, :, :, cut], turned_ref, outs, (r, c), cut, y, z)


def relayout_high(high, sizes):
    rows, two, colours, slices, count = high.shape
    return pl.pallas_call(
        relayout_high_body,
        in_specs=[pl.BlockSpec(memory_space=pl.ANY)],
        out_specs=[VMEM] * (len(sizes) + 1),
        out_shape=[pltpu.VMEM((n, two, colours, rows, count), jnp.bfloat16) for n in sizes]
        + [TOKEN],
        scratch_shapes=[
            pltpu.VMEM((two * colours, rows, slices, count), jnp.bfloat16),
            pltpu.VMEM((slices, rows, STEP), jnp.bfloat16),
            pltpu.SemaphoreType.DMA((two * colours,)),
        ],
        compiler_params=pltpu.CompilerParams(vmem_limit_bytes=HIGH_LIMIT),
        cost_estimate=TINY,
        name="relayout_high",
    )(stay(high))


def relayout_low_body(in_ref, after_ref, many_ref, few_ref, token_ref, turned_ref):
    _, y, z = coords()
    token_ref[...] = jnp.zeros_like(token_ref)

    def one(s, carry):
        for j in range(0, in_ref.shape[-1], STEP):
            cut = pl.ds(j, STEP)
            values = in_ref[:, s, 0, 0, :, cut]
            turn(values, turned_ref, (many_ref, few_ref), (0, 0, s), cut, y, z)
        return carry

    lax.fori_loop(0, in_ref.shape[1], one, 0)


def relayout_low(low, after, sizes):
    rows, spins, two, colours, slices, count = low.shape
    *turned, token = pl.pallas_call(
        relayout_low_body,
        grid=(colours, two),
        in_specs=[
            pl.BlockSpec((rows, spins, 1, 1, slices, count), lambda c, u: (0, 0, u, c, 0, 0)),
            whole((8, 128)),
        ],
        out_specs=[
            pl.BlockSpec((n, 1, 1, spins, rows, count), lambda c, u: (0, c, u, 0, 0, 0))
            for n in sizes
        ]
        + [whole((8, 128))],
        out_shape=[
            space((n, colours, two, spins, rows, count), jnp.bfloat16)
            for n, space in zip(sizes, (pltpu.HBM, pltpu.VMEM))
        ]
        + [TOKEN],
        scratch_shapes=[pltpu.VMEM((slices, rows, STEP), jnp.bfloat16)],
        compiler_params=pltpu.CompilerParams(vmem_limit_bytes=LOW_LIMIT),
        cost_estimate=TINY,
        name="relayout_low",
    )(stay(low), after)
    turned = [t.reshape(t.shape[0], colours, two * spins * rows, count) for t in turned]
    return turned, token


def contract_body(by_part, blocks, based, added, pat_ref, cos_ref, sin_ref, own_ref, oth_ref, *refs):
    highs, refs = refs[: len(blocks)], refs[len(blocks) :]
    base_ref, refs = (refs[0], refs[1:]) if based else (None, refs)
    adds, outs = refs[:added], refs[1 + added : -2]
    token_ref, acc_ref = refs[-2:]
    token_ref[...] = jnp.zeros_like(token_ref)
    n_moms, count = cos_ref.shape
    x, _, _ = coords()
    acc_ref[...] = jnp.zeros_like(acc_ref)

    def one(colour, carry):
        total = None
        for j in range(0, count, STEP):
            cut = pl.ds(j, STEP)
            rows = []
            for high_ref in highs:
                real = high_ref[0, 0, colour, :, cut].astype(jnp.float32)
                imag = high_ref[0, 1, colour, :, cut].astype(jnp.float32)
                reals, imags = [], []
                for p in range(n_moms):
                    cosine = cos_ref[p : p + 1, cut]
                    sine = sin_ref[p : p + 1, cut]
                    reals.append((real * cosine - imag * sine).astype(jnp.bfloat16))
                    imags.append((real * sine + imag * cosine).astype(jnp.bfloat16))
                rows += reals + imags
            phased = jnp.concatenate(rows, 0)
            low = jnp.concatenate([own_ref[0, colour, :, cut], oth_ref[0, colour, :, cut]], 0)
            part = lax.dot_general(
                low, phased, (((1,), (1,)), ((), ())), preferred_element_type=jnp.float32
            )
            total = part if total is None else total + part
        acc_ref[...] += total
        return carry

    lax.fori_loop(0, 3, one, 0)
    half = 128

    def put(k, block, result):
        for add in adds:
            result = result + add[add.shape[0] - 1, k, block].astype(jnp.float32)
        if by_part:
            outs[k // 2][k % 2, 0, block] = result.astype(outs[k // 2].dtype)
        else:
            outs[0][0, k, block] = result.astype(outs[0].dtype)

    if based:
        for k in range(NX):
            put(k, 0, base_ref[0, k, 0])
    for place, block in enumerate(blocks):
        base = place * 256
        pattern = pat_ref[0:1, block * half : block * half + half]
        is_spin = [jnp.broadcast_to(pattern == a, (16, half)) for a in range(4)]
        low_pair = pattern < 2
        odd = jnp.logical_or(pattern == 1, pattern == 3)
        mesons = [[], [], [], []]
        for owner in range(2):
            over = []
            for s in range(4):
                u0 = slice(owner * 128 + s * 16, owner * 128 + s * 16 + 16)
                u1 = slice(owner * 128 + s * 16 + 64, owner * 128 + s * 16 + 80)
                r0, r1 = slice(base, base + half), slice(base + half, base + 2 * half)
                over.append((acc_ref[u0, r0] + acc_ref[u1, r1], acc_ref[u1, r0] - acc_ref[u0, r1]))
            for g in range(4):
                picked = []
                for u in range(2):
                    value = over[PARTNER[g][3]][u]
                    for a in range(3):
                        value = jnp.where(is_spin[a], over[PARTNER[g][a]][u], value)
                    picked.append(value)
                re, im = picked
                if g == 2:
                    re, im = jnp.where(low_pair, -im, im), jnp.where(low_pair, re, -re)
                if g == 3:
                    re, im = jnp.where(odd, re, -re), jnp.where(odd, im, -im)
                mesons[g] += [re, im]
        stacked = [jnp.concatenate(m, 0) for m in mesons]
        lane = lax.broadcasted_iota(jnp.int32, stacked[0].shape, 1) // 32
        for k in range(NX):
            group = x ^ OWNERS[k]
            result = None
            for g in range(4):
                turned = pltpu.roll(stacked[g], lax.rem(g - group + NX, NX) * 32, 1)
                result = turned if result is None else jnp.where(lane == g, turned, result)
            put(k, block, result)


def contract(tables, lows, own, received, first, by_part, sent, after, limit, adds=(), base=None):
    colours, rows, count = lows[0].shape[1:]
    highs = [h for h in (own, received) if h is not None]
    blocks = tuple(b for b, h in enumerate((own, received)) if h is not None)
    number = highs[0].shape[0]
    unit = (1 if received is None else 2, 64, 128)
    if by_part:
        shapes = [
            jax.ShapeDtypeStruct((2, number) + unit, sent),
            jax.ShapeDtypeStruct((2, number) + unit, jnp.float32),
        ]
        out_specs = [pl.BlockSpec((2, 1) + unit, lambda i: (0, i, 0, 0, 0))] * 2
    else:
        shapes = [jax.ShapeDtypeStruct((number, NX) + unit, sent)]
        out_specs = [pl.BlockSpec((1, NX) + unit, lambda i: (i, 0, 0, 0, 0))]
    high_spec = pl.BlockSpec((1, 2, colours, 16, count), lambda i: (i, 0, 0, 0, 0))
    low_spec = pl.BlockSpec((1, colours, rows, count), lambda i: (first + i, 0, 0, 0))
    extra = list(adds) if base is None else [base, *adds]
    return pl.pallas_call(
        functools.partial(contract_body, by_part, blocks, base is not None, len(adds)),
        grid=(number,),
        in_specs=[whole(t.shape) for t in tables]
        + [low_spec, low_spec]
        + [high_spec] * len(highs)
        + [whole(a.shape) for a in extra]
        + [whole((8, 128))],
        out_specs=out_specs + [whole((8, 128))],
        out_shape=shapes + [TOKEN],
        scratch_shapes=[pltpu.VMEM((256, 256 * len(highs)), jnp.float32)],
        compiler_params=pltpu.CompilerParams(vmem_limit_bytes=limit),
        cost_estimate=TINY,
        name=f"contract_{first}_{number}",
    )(*tables, *lows, *highs, *extra, after)


def fold_body(number, *refs):
    parts, (first_ref, second_ref, token_ref) = refs[:number], refs[-3:]
    half = parts[0].shape[0] // 2
    for out_ref, cut in ((first_ref, slice(0, half)), (second_ref, slice(half, 2 * half))):
        total = None
        for part in parts:
            value = part[cut].astype(jnp.float32)
            total = value if total is None else total + value
        out_ref[...] = total.astype(out_ref.dtype)
    token_ref[...] = jnp.zeros_like(token_ref)


def fold(parts, sent, after):
    shape = (parts[0].shape[0] // 2,) + parts[0].shape[1:]
    return pl.pallas_call(
        functools.partial(fold_body, len(parts)),
        in_specs=[VMEM] * (len(parts) + 1),
        out_specs=[VMEM] * 3,
        out_shape=[
            jax.ShapeDtypeStruct(shape, sent),
            jax.ShapeDtypeStruct(shape, jnp.float32),
            TOKEN,
        ],
        compiler_params=SMALL,
        cost_estimate=TINY,
        name="fold",
    )(*parts, after)


def plus_body(number, *refs):
    parts, out_ref, token_ref = refs[:number], refs[-2], refs[-1]
    total = None
    for part in parts:
        value = part[: out_ref.shape[0]].astype(jnp.float32)
        total = value if total is None else total + value
    out_ref[...] = total.astype(out_ref.dtype)
    token_ref[...] = jnp.zeros_like(token_ref)


def plus(parts, sent, after):
    length = min(part.shape[0] for part in parts)
    return pl.pallas_call(
        functools.partial(plus_body, len(parts)),
        in_specs=[VMEM] * (len(parts) + 1),
        out_specs=[VMEM] * 2,
        out_shape=[jax.ShapeDtypeStruct((length,) + parts[0].shape[1:], sent), TOKEN],
        compiler_params=SMALL,
        cost_estimate=TINY,
        name="plus",
    )(*parts, after)


def finish_body(kept_ref, last_ref, across_ref, mine_ref, other_ref):
    for out_ref, rows in ((mine_ref, slice(0, 32)), (other_ref, slice(32, 64))):
        out_ref[...] = kept_ref[0, :, rows] + last_ref[0, :, rows].astype(jnp.float32) + across_ref[0, :, rows]


def finish(kept, last, across):
    return pl.pallas_call(
        finish_body,
        in_specs=[VMEM] * 3,
        out_specs=[VMEM] * 2,
        out_shape=[jax.ShapeDtypeStruct((2, 32, 128), jnp.float32)] * 2,
        compiler_params=SMALL,
        cost_estimate=TINY,
        name="finish",
    )(kept, last, across)


def assemble_body(mine_ref, other_ref, out_ref):
    mode = lax.axis_index("mode")
    blocks = [mode, mode ^ 2, mode ^ 1, mode ^ 3]
    lane = lax.broadcasted_iota(jnp.int32, (32, 128), 1) // 16
    held = [mine_ref[0], mine_ref[1], other_ref[0], other_ref[1]]
    for g in range(4):
        for p in range(2):
            result = None
            for values, block in zip(held, blocks):
                shift = lax.rem(block * 16 - (g * 32 + p * 16) + 128, 128)
                turned = pltpu.roll(values, shift, 1)
                result = turned if result is None else jnp.where(lane == block, turned, result)
            for u in range(2):
                out_ref[g, u, p] = result[u * 16 : u * 16 + 16, :64]


def assemble(pieces):
    return pl.pallas_call(
        assemble_body,
        out_shape=jax.ShapeDtypeStruct((4, 2, 2, 16, 64), jnp.float32),
        compiler_params=SMALL,
        cost_estimate=TINY,
        name="assemble",
    )(*pieces)


def phase_tables(momenta, first_site, count):
    sites = first_site + jnp.arange(count, dtype=jnp.int32)
    coords = jnp.stack([sites % 32, sites // 32 % 32, sites // 1024])
    turns = jnp.sum(momenta[:, :, None] * coords[None, :, :], axis=1)
    angles = turns.astype(jnp.float32) * (2.0 * math.pi / 96.0)
    return jnp.cos(angles), jnp.sin(angles)


def body(low_modes, high_modes, pattern, momenta):
    count = low_modes.shape[-1]
    my_mode = lax.axis_index("mode")
    wide, narrow = jnp.float32, jnp.bfloat16
    *high, token = relayout_high(high_modes, (2, 2, 2, 1, 1))
    arrived = [flip(chunk, 2) for chunk in high]
    gated, token = lax.optimization_barrier((low_modes, token))
    low_oth = flip(gated, 1)
    low_own, token = relayout_low(low_modes, token, (4, 4))
    low_oth, token = relayout_low(low_oth, token, (4, 4))
    many, few = zip(low_own, low_oth)
    many = [stay(a) for a in many]
    cosines, sines = phase_tables(momenta, lax.axis_index("site") * count, count)

    def lanes(block):
        part = lax.dynamic_slice_in_dim(pattern, block * 16, 16, 0)
        return jnp.broadcast_to(jnp.tile(part, 8)[None, :], (8, 128))

    tables = (jnp.concatenate([lanes(my_mode), lanes(my_mode ^ 2)], 1), cosines, sines)
    away, token = contract(
        tables, many, high[0], arrived[0], 0, False, narrow, token, MANY_LIMIT
    )
    far_got = trade(away, 1, 0, 0)
    far, token = contract(
        tables, many, high[1], arrived[1], 2, False, wide, token, MANY_LIMIT
    )
    away, far, token = fold((far, far_got), narrow, token)
    far_got = trade(away, 3, 0, 0)
    base, token = contract(tables, few, high[3], None, 2, False, wide, token, FEW_LIMIT)
    away, far, token = fold((far[0], far_got[0]), narrow, token)
    far_got = trade(away, 0, 0, 1)
    last_base, token = contract(tables, few, high[4], None, 3, False, wide, token, FEW_LIMIT)
    away, far, token = fold((far, far_got), narrow, token)
    far_got = trade(away, 0, 0, 3)
    away, token = contract(
        tables, few, high[2], arrived[2], 0, False, narrow, token, FEW_LIMIT
    )
    near_got = trade(away, 1, 0, 0)
    near, token = contract(
        tables, few, None, arrived[3], 2, False, wide, token, FEW_LIMIT, (), base
    )
    away, token = plus((far, far_got), wide, token)
    across = trade(away, 0, 1, 0)
    away, token = plus((near, near_got), narrow, token)
    adds = (near_got, trade(away, 3, 0, 0))
    away, near, token = contract(
        tables, few, None, arrived[4], 3, True, narrow, token, FEW_LIMIT, adds, last_base
    )
    last_got = trade(away, 0, 0, 1)
    away, near, token = fold((near[:, 0], last_got[:, 0]), narrow, token)
    last_got = trade(away, 0, 0, 3)
    mine, other = finish(near, last_got, across)
    pieces = (mine, flip(other, 1))
    return jnp.transpose(assemble(pieces), (0, 1, 2, 4, 3))


def solution(mesh):
    placed = (
        P("mode", None, None, None, None, "site"),
        P("mode", None, None, None, "site"),
        P(),
        P(),
    )
    return jax.shard_map(
        body,
        mesh=mesh,
        in_specs=placed,
        out_specs=P(None, None, "site", None, "mode"),
        check_vma=False,
    )
```

```python
import functools
import math

import jax
import jax.numpy as jnp
from jax import lax
from jax.experimental import pallas as pl
from jax.experimental.pallas import tpu as pltpu
from jax.sharding import PartitionSpec as P

NX, NY, NZ = 4, 4, 2
SLOTS = NY * NZ
PARTNER = ((0, 1, 2, 3), (2, 3, 0, 1), (3, 2, 1, 0), (1, 0, 3, 2))
OWNERS = (2, 1, 3, 0)


def coords():
    site = lax.axis_index("site")
    return lax.rem(site, 4), lax.div(site, 8), lax.rem(lax.div(site, 4), 2)


def site_of(y, z, x):
    return ((y % NY) * NZ + z % NZ) * NX + x % NX


def trade(block, ymask, zmask, xmask):
    route = [
        (site_of(y, z, x), site_of(y ^ ymask, z ^ zmask, x ^ xmask))
        for y in range(NY)
        for z in range(NZ)
        for x in range(NX)
    ]
    return lax.ppermute(block, "site", route)


def flip(block, mask):
    return lax.ppermute(block, "mode", [(i, i ^ mask) for i in range(4)])


def slot_of(t, y, z):
    far = (t // 2) ^ y
    place = jnp.where(far == 2, 0, jnp.where(far == 1, 1, jnp.where(far == 3, 2, 3)))
    return jnp.where(t % 2 == z, NY, 0) + place


def time_of(slot, y, z):
    plane = z if slot >= NY else 1 - z
    return 2 * (y ^ OWNERS[slot % NY]) + plane


VMEM = pl.BlockSpec(memory_space=pltpu.VMEM)
STEP = 512
HIGH_LIMIT = 12 * 2**20
LOW_LIMIT = 16 * 2**20
MANY_LIMIT = 24 * 2**20
FEW_LIMIT = 14 * 2**20
SMALL = pltpu.CompilerParams(vmem_limit_bytes=4 * 2**20)
TOKEN = jax.ShapeDtypeStruct((8, 128), jnp.float32)
TINY = pl.CostEstimate(flops=0, bytes_accessed=0, transcendentals=0)


def stay(array):
    return pltpu.with_memory_space_constraint(array, pltpu.HBM)


def whole(shape):
    return pl.BlockSpec(shape, lambda *_: (0,) * len(shape))


def turn(values, turned_ref, outs, index, cut, y, z):
    turned_ref[...] = jnp.swapaxes(values, 0, 1)
    slot = 0
    for out in outs:
        for k in range(out.shape[0]):
            out[(k,) + index + (slice(None), cut)] = turned_ref[time_of(slot, y, z)]
            slot += 1


def relayout_high_body(in_ref, *refs):
    outs, (token_ref, held_ref, turned_ref, sems) = refs[:-4], refs[-4:]
    _, y, z = coords()
    token_ref[...] = jnp.zeros_like(token_ref)
    pieces = [(r, c) for r in range(2) for c in range(3)]
    copies = [
        pltpu.make_async_copy(in_ref.at[:, r, c], held_ref.at[i], sems.at[i])
        for i, (r, c) in enumerate(pieces)
    ]
    for copy in copies:
        copy.start()
    for i, (r, c) in enumerate(pieces):
        copies[i].wait()
        for j in range(0, held_ref.shape[-1], STEP):
            cut = pl.ds(j, STEP)
            turn(held_ref[i, :, :, cut], turned_ref, outs, (r, c), cut, y, z)


def relayout_high(high, sizes):
    rows, two, colours, slices, count = high.shape
    return pl.pallas_call(
        relayout_high_body,
        in_specs=[pl.BlockSpec(memory_space=pl.ANY)],
        out_specs=[VMEM] * (len(sizes) + 1),
        out_shape=[pltpu.VMEM((n, two, colours, rows, count), jnp.bfloat16) for n in sizes]
        + [TOKEN],
        scratch_shapes=[
            pltpu.VMEM((two * colours, rows, slices, count), jnp.bfloat16),
            pltpu.VMEM((slices, rows, STEP), jnp.bfloat16),
            pltpu.SemaphoreType.DMA((two * colours,)),
        ],
        compiler_params=pltpu.CompilerParams(vmem_limit_bytes=HIGH_LIMIT),
        cost_estimate=TINY,
        name="relayout_high",
    )(stay(high))


def relayout_low_body(in_ref, after_ref, many_ref, few_ref, token_ref, turned_ref):
    _, y, z = coords()
    token_ref[...] = jnp.zeros_like(token_ref)

    def one(s, carry):
        for j in range(0, in_ref.shape[-1], STEP):
            cut = pl.ds(j, STEP)
            values = in_ref[:, s, 0, 0, :, cut]
            turn(values, turned_ref, (many_ref, few_ref), (0, 0, s), cut, y, z)
        return carry

    lax.fori_loop(0, in_ref.shape[1], one, 0)


def relayout_low(low, after, sizes):
    rows, spins, two, colours, slices, count = low.shape
    *turned, token = pl.pallas_call(
        relayout_low_body,
        grid=(colours, two),
        in_specs=[
            pl.BlockSpec((rows, spins, 1, 1, slices, count), lambda c, u: (0, 0, u, c, 0, 0)),
            whole((8, 128)),
        ],
        out_specs=[
            pl.BlockSpec((n, 1, 1, spins, rows, count), lambda c, u: (0, c, u, 0, 0, 0))
            for n in sizes
        ]
        + [whole((8, 128))],
        out_shape=[
            space((n, colours, two, spins, rows, count), jnp.bfloat16)
            for n, space in zip(sizes, (pltpu.HBM, pltpu.VMEM))
        ]
        + [TOKEN],
        scratch_shapes=[pltpu.VMEM((slices, rows, STEP), jnp.bfloat16)],
        compiler_params=pltpu.CompilerParams(vmem_limit_bytes=LOW_LIMIT),
        cost_estimate=TINY,
        name="relayout_low",
    )(stay(low), after)
    turned = [t.reshape(t.shape[0], colours, two * spins * rows, count) for t in turned]
    return turned, token


def contract_body(by_part, blocks, based, added, pat_ref, cos_ref, sin_ref, own_ref, oth_ref, *refs):
    highs, refs = refs[: len(blocks)], refs[len(blocks) :]
    base_ref, refs = (refs[0], refs[1:]) if based else (None, refs)
    adds, outs = refs[:added], refs[1 + added : -2]
    token_ref, acc_ref = refs[-2:]
    token_ref[...] = jnp.zeros_like(token_ref)
    n_moms, count = cos_ref.shape
    x, _, _ = coords()
    acc_ref[...] = jnp.zeros_like(acc_ref)

    def one(colour, carry):
        total = None
        for j in range(0, count, STEP):
            cut = pl.ds(j, STEP)
            rows = []
            for high_ref in highs:
                real = high_ref[0, 0, colour, :, cut].astype(jnp.float32)
                imag = high_ref[0, 1, colour, :, cut].astype(jnp.float32)
                reals, imags = [], []
                for p in range(n_moms):
                    cosine = cos_ref[p : p + 1, cut]
                    sine = sin_ref[p : p + 1, cut]
                    reals.append((real * cosine - imag * sine).astype(jnp.bfloat16))
                    imags.append((real * sine + imag * cosine).astype(jnp.bfloat16))
                rows += reals + imags
            phased = jnp.concatenate(rows, 0)
            low = jnp.concatenate([own_ref[0, colour, :, cut], oth_ref[0, colour, :, cut]], 0)
            part = lax.dot_general(
                low, phased, (((1,), (1,)), ((), ())), preferred_element_type=jnp.float32
            )
            total = part if total is None else total + part
        acc_ref[...] += total
        return carry

    lax.fori_loop(0, 3, one, 0)
    half = 128

    def put(k, block, result):
        for add in adds:
            result = result + add[add.shape[0] - 1, k, block].astype(jnp.float32)
        if by_part:
            outs[k // 2][k % 2, 0, block] = result.astype(outs[k // 2].dtype)
        else:
            outs[0][0, k, block] = result.astype(outs[0].dtype)

    if based:
        for k in range(NX):
            put(k, 0, base_ref[0, k, 0])
    for place, block in enumerate(blocks):
        base = place * 256
        pattern = pat_ref[0:1, block * half : block * half + half]
        is_spin = [jnp.broadcast_to(pattern == a, (16, half)) for a in range(4)]
        low_pair = pattern < 2
        odd = jnp.logical_or(pattern == 1, pattern == 3)
        mesons = [[], [], [], []]
        for owner in range(2):
            over = []
            for s in range(4):
                u0 = slice(owner * 128 + s * 16, owner * 128 + s * 16 + 16)
                u1 = slice(owner * 128 + s * 16 + 64, owner * 128 + s * 16 + 80)
                r0, r1 = slice(base, base + half), slice(base + half, base + 2 * half)
                over.append((acc_ref[u0, r0] + acc_ref[u1, r1], acc_ref[u1, r0] - acc_ref[u0, r1]))
            for g in range(4):
                picked = []
                for u in range(2):
                    value = over[PARTNER[g][3]][u]
                    for a in range(3):
                        value = jnp.where(is_spin[a], over[PARTNER[g][a]][u], value)
                    picked.append(value)
                re, im = picked
                if g == 2:
                    re, im = jnp.where(low_pair, -im, im), jnp.where(low_pair, re, -re)
                if g == 3:
                    re, im = jnp.where(odd, re, -re), jnp.where(odd, im, -im)
                mesons[g] += [re, im]
        stacked = [jnp.concatenate(m, 0) for m in mesons]
        lane = lax.broadcasted_iota(jnp.int32, stacked[0].shape, 1) // 32
        for k in range(NX):
            group = x ^ OWNERS[k]
            result = None
            for g in range(4):
                turned = pltpu.roll(stacked[g], lax.rem(g - group + NX, NX) * 32, 1)
                result = turned if result is None else jnp.where(lane == g, turned, result)
            put(k, block, result)


def contract(tables, lows, own, received, first, by_part, sent, after, limit, adds=(), base=None):
    colours, rows, count = lows[0].shape[1:]
    highs = [h for h in (own, received) if h is not None]
    blocks = tuple(b for b, h in enumerate((own, received)) if h is not None)
    number = highs[0].shape[0]
    unit = (1 if received is None else 2, 64, 128)
    if by_part:
        shapes = [
            jax.ShapeDtypeStruct((2, number) + unit, sent),
            jax.ShapeDtypeStruct((2, number) + unit, jnp.float32),
        ]
        out_specs = [pl.BlockSpec((2, 1) + unit, lambda i: (0, i, 0, 0, 0))] * 2
    else:
        shapes = [jax.ShapeDtypeStruct((number, NX) + unit, sent)]
        out_specs = [pl.BlockSpec((1, NX) + unit, lambda i: (i, 0, 0, 0, 0))]
    high_spec = pl.BlockSpec((1, 2, colours, 16, count), lambda i: (i, 0, 0, 0, 0))
    low_spec = pl.BlockSpec((1, colours, rows, count), lambda i: (first + i, 0, 0, 0))
    extra = list(adds) if base is None else [base, *adds]
    return pl.pallas_call(
        functools.partial(contract_body, by_part, blocks, base is not None, len(adds)),
        grid=(number,),
        in_specs=[whole(t.shape) for t in tables]
        + [low_spec, low_spec]
        + [high_spec] * len(highs)
        + [whole(a.shape) for a in extra]
        + [whole((8, 128))],
        out_specs=out_specs + [whole((8, 128))],
        out_shape=shapes + [TOKEN],
        scratch_shapes=[pltpu.VMEM((256, 256 * len(highs)), jnp.float32)],
        compiler_params=pltpu.CompilerParams(vmem_limit_bytes=limit),
        cost_estimate=TINY,
        name=f"contract_{first}_{number}",
    )(*tables, *lows, *highs, *extra, after)


def fold_body(number, *refs):
    parts, (first_ref, second_ref, token_ref) = refs[:number], refs[-3:]
    half = parts[0].shape[0] // 2
    for out_ref, cut in ((first_ref, slice(0, half)), (second_ref, slice(half, 2 * half))):
        total = None
        for part in parts:
            value = part[cut].astype(jnp.float32)
            total = value if total is None else total + value
        out_ref[...] = total.astype(out_ref.dtype)
    token_ref[...] = jnp.zeros_like(token_ref)


def fold(parts, sent, after):
    shape = (parts[0].shape[0] // 2,) + parts[0].shape[1:]
    return pl.pallas_call(
        functools.partial(fold_body, len(parts)),
        in_specs=[VMEM] * (len(parts) + 1),
        out_specs=[VMEM] * 3,
        out_shape=[
            jax.ShapeDtypeStruct(shape, sent),
            jax.ShapeDtypeStruct(shape, jnp.float32),
            TOKEN,
        ],
        compiler_params=SMALL,
        cost_estimate=TINY,
        name="fold",
    )(*parts, after)


def plus_body(number, *refs):
    parts, out_ref, token_ref = refs[:number], refs[-2], refs[-1]
    total = None
    for part in parts:
        value = part[: out_ref.shape[0]].astype(jnp.float32)
        total = value if total is None else total + value
    out_ref[...] = total.astype(out_ref.dtype)
    token_ref[...] = jnp.zeros_like(token_ref)


def plus(parts, sent, after):
    length = min(part.shape[0] for part in parts)
    return pl.pallas_call(
        functools.partial(plus_body, len(parts)),
        in_specs=[VMEM] * (len(parts) + 1),
        out_specs=[VMEM] * 2,
        out_shape=[jax.ShapeDtypeStruct((length,) + parts[0].shape[1:], sent), TOKEN],
        compiler_params=SMALL,
        cost_estimate=TINY,
        name="plus",
    )(*parts, after)


def finish_body(kept_ref, last_ref, across_ref, mine_ref, other_ref):
    for out_ref, rows in ((mine_ref, slice(0, 32)), (other_ref, slice(32, 64))):
        out_ref[...] = kept_ref[0, :, rows] + last_ref[0, :, rows].astype(jnp.float32) + across_ref[0, :, rows]


def finish(kept, last, across):
    return pl.pallas_call(
        finish_body,
        in_specs=[VMEM] * 3,
        out_specs=[VMEM] * 2,
        out_shape=[jax.ShapeDtypeStruct((2, 32, 128), jnp.float32)] * 2,
        compiler_params=SMALL,
        cost_estimate=TINY,
        name="finish",
    )(kept, last, across)


def assemble_body(mine_ref, other_ref, out_ref):
    mode = lax.axis_index("mode")
    blocks = [mode, mode ^ 2, mode ^ 1, mode ^ 3]
    lane = lax.broadcasted_iota(jnp.int32, (32, 128), 1) // 16
    held = [mine_ref[0], mine_ref[1], other_ref[0], other_ref[1]]
    for g in range(4):
        for p in range(2):
            result = None
            for values, block in zip(held, blocks):
                shift = lax.rem(block * 16 - (g * 32 + p * 16) + 128, 128)
                turned = pltpu.roll(values, shift, 1)
                result = turned if result is None else jnp.where(lane == block, turned, result)
            for u in range(2):
                out_ref[g, u, p] = result[u * 16 : u * 16 + 16, :64]


def assemble(pieces):
    return pl.pallas_call(
        assemble_body,
        out_shape=jax.ShapeDtypeStruct((4, 2, 2, 16, 64), jnp.float32),
        compiler_params=SMALL,
        cost_estimate=TINY,
        name="assemble",
    )(*pieces)


def phase_tables(momenta, first_site, count):
    sites = first_site + jnp.arange(count, dtype=jnp.int32)
    coords = jnp.stack([sites % 32, sites // 32 % 32, sites // 1024])
    turns = jnp.sum(momenta[:, :, None] * coords[None, :, :], axis=1)
    angles = turns.astype(jnp.float32) * (2.0 * math.pi / 96.0)
    return jnp.cos(angles), jnp.sin(angles)


def body(low_modes, high_modes, pattern, momenta):
    count = low_modes.shape[-1]
    my_mode = lax.axis_index("mode")
    wide, narrow = jnp.float32, jnp.bfloat16
    *high, token = relayout_high(high_modes, (2, 2, 2, 1, 1))
    arrived = [flip(chunk, 2) for chunk in high]
    gated, token = lax.optimization_barrier((low_modes, token))
    low_oth = flip(gated, 1)
    low_own, token = relayout_low(low_modes, token, (4, 4))
    low_oth, token = relayout_low(low_oth, token, (4, 4))
    many, few = zip(low_own, low_oth)
    many = [stay(a) for a in many]
    cosines, sines = phase_tables(momenta, lax.axis_index("site") * count, count)

    def lanes(block):
        part = lax.dynamic_slice_in_dim(pattern, block * 16, 16, 0)
        return jnp.broadcast_to(jnp.tile(part, 8)[None, :], (8, 128))

    tables = (jnp.concatenate([lanes(my_mode), lanes(my_mode ^ 2)], 1), cosines, sines)
    away, token = contract(
        tables, many, high[0], arrived[0], 0, False, narrow, token, MANY_LIMIT
    )
    far_got = trade(away, 1, 0, 0)
    far, token = contract(
        tables, many, high[1], arrived[1], 2, False, wide, token, MANY_LIMIT
    )
    away, far, token = fold((far, far_got), narrow, token)
    far_got = trade(away, 3, 0, 0)
    base, token = contract(tables, few, high[3], None, 2, False, wide, token, FEW_LIMIT)
    away, far, token = fold((far[0], far_got[0]), narrow, token)
    far_got = trade(away, 0, 0, 1)
    last_base, token = contract(tables, few, high[4], None, 3, False, wide, token, FEW_LIMIT)
    away, far, token = fold((far, far_got), narrow, token)
    far_got = trade(away, 0, 0, 3)
    away, token = contract(
        tables, few, high[2], arrived[2], 0, False, narrow, token, FEW_LIMIT
    )
    near_got = trade(away, 1, 0, 0)
    near, token = contract(
        tables, few, None, arrived[3], 2, False, wide, token, FEW_LIMIT, (), base
    )
    away, token = plus((far, far_got), wide, token)
    across = trade(away, 0, 1, 0)
    away, token = plus((near, near_got), narrow, token)
    near_last = trade(away, 3, 0, 0)
    near, token = contract(
        tables, few, None, arrived[4], 3, False, wide, token, FEW_LIMIT, (near_got,), last_base
    )
    away, near, token = fold((near[0], near_last[0]), narrow, token)
    last_got = trade(away, 0, 0, 1)
    away, near, token = fold((near, last_got), narrow, token)
    last_got = trade(away, 0, 0, 3)
    mine, other = finish(near, last_got, across)
    pieces = (mine, flip(other, 1))
    return jnp.transpose(assemble(pieces), (0, 1, 2, 4, 3))


def solution(mesh):
    placed = (
        P("mode", None, None, None, None, "site"),
        P("mode", None, None, None, "site"),
        P(),
        P(),
    )
    return jax.shard_map(
        body,
        mesh=mesh,
        in_specs=placed,
        out_specs=P(None, None, "site", None, "mode"),
        check_vma=False,
    )
```

```python
import functools
import math

import jax
import jax.numpy as jnp
from jax import lax
from jax.experimental import pallas as pl
from jax.experimental.pallas import tpu as pltpu
from jax.sharding import PartitionSpec as P

NX, NY, NZ = 4, 4, 2
SLOTS = NY * NZ
PARTNER = ((0, 1, 2, 3), (2, 3, 0, 1), (3, 2, 1, 0), (1, 0, 3, 2))
OWNERS = (2, 1, 3, 0)


def coords():
    site = lax.axis_index("site")
    return lax.rem(site, 4), lax.div(site, 8), lax.rem(lax.div(site, 4), 2)


def site_of(y, z, x):
    return ((y % NY) * NZ + z % NZ) * NX + x % NX


def trade(block, ymask, zmask, xmask):
    route = [
        (site_of(y, z, x), site_of(y ^ ymask, z ^ zmask, x ^ xmask))
        for y in range(NY)
        for z in range(NZ)
        for x in range(NX)
    ]
    return lax.ppermute(block, "site", route)


def flip(block, mask):
    return lax.ppermute(block, "mode", [(i, i ^ mask) for i in range(4)])


def slot_of(t, y, z):
    far = (t // 2) ^ y
    place = jnp.where(far == 2, 0, jnp.where(far == 1, 1, jnp.where(far == 3, 2, 3)))
    return jnp.where(t % 2 == z, NY, 0) + place


def time_of(slot, y, z):
    plane = z if slot >= NY else 1 - z
    return 2 * (y ^ OWNERS[slot % NY]) + plane


VMEM = pl.BlockSpec(memory_space=pltpu.VMEM)
STEP = 512
HIGH_LIMIT = 6 * 2**20
LOW_LIMIT = 10 * 2**20
MANY_LIMIT = 14 * 2**20
FEW_LIMIT = 14 * 2**20
SMALL = pltpu.CompilerParams(vmem_limit_bytes=4 * 2**20)
TOKEN = jax.ShapeDtypeStruct((8, 128), jnp.float32)
TINY = pl.CostEstimate(flops=0, bytes_accessed=0, transcendentals=0)


def stay(array):
    return pltpu.with_memory_space_constraint(array, pltpu.HBM)


def whole(shape):
    return pl.BlockSpec(shape, lambda *_: (0,) * len(shape))


def turn(values, turned_ref, outs, index, cut, y, z):
    turned_ref[...] = jnp.swapaxes(values, 0, 1)
    slot = 0
    for out in outs:
        for k in range(out.shape[0]):
            out[(k,) + index + (slice(None), cut)] = turned_ref[time_of(slot, y, z)]
            slot += 1


def relayout_high_body(in_ref, *refs):
    outs, (token_ref, held_ref, turned_ref, sems) = refs[:-4], refs[-4:]
    _, y, z = coords()
    token_ref[...] = jnp.zeros_like(token_ref)
    pieces = [(r, c) for r in range(2) for c in range(3)]
    copies = [
        pltpu.make_async_copy(in_ref.at[:, r, c], held_ref.at[i], sems.at[i])
        for i, (r, c) in enumerate(pieces)
    ]
    for copy in copies:
        copy.start()
    for i, (r, c) in enumerate(pieces):
        copies[i].wait()
        for j in range(0, held_ref.shape[-1], STEP):
            cut = pl.ds(j, STEP)
            turn(held_ref[i, :, :, cut], turned_ref, outs, (r, c), cut, y, z)


def relayout_high(high, sizes):
    rows, two, colours, slices, count = high.shape
    return pl.pallas_call(
        relayout_high_body,
        in_specs=[pl.BlockSpec(memory_space=pl.ANY)],
        out_specs=[VMEM] * (len(sizes) + 1),
        out_shape=[pltpu.VMEM((n, two, colours, rows, count), jnp.bfloat16) for n in sizes]
        + [TOKEN],
        scratch_shapes=[
            pltpu.VMEM((two * colours, rows, slices, count), jnp.bfloat16),
            pltpu.VMEM((slices, rows, STEP), jnp.bfloat16),
            pltpu.SemaphoreType.DMA((two * colours,)),
        ],
        compiler_params=pltpu.CompilerParams(vmem_limit_bytes=HIGH_LIMIT),
        cost_estimate=TINY,
        name="relayout_high",
    )(stay(high))


def relayout_low_body(in_ref, after_ref, many_ref, few_ref, token_ref, turned_ref):
    _, y, z = coords()
    token_ref[...] = jnp.zeros_like(token_ref)

    def one(s, carry):
        for j in range(0, in_ref.shape[-1], STEP):
            cut = pl.ds(j, STEP)
            values = in_ref[:, s, 0, 0, :, cut]
            turn(values, turned_ref, (many_ref, few_ref), (0, 0, s), cut, y, z)
        return carry

    lax.fori_loop(0, in_ref.shape[1], one, 0)


def relayout_low(low, after, sizes):
    rows, spins, two, colours, slices, count = low.shape
    *turned, token = pl.pallas_call(
        relayout_low_body,
        grid=(colours, two),
        in_specs=[
            pl.BlockSpec((rows, spins, 1, 1, slices, count), lambda c, u: (0, 0, u, c, 0, 0)),
            whole((8, 128)),
        ],
        out_specs=[
            pl.BlockSpec((n, 1, 1, spins, rows, count), lambda c, u: (0, c, u, 0, 0, 0))
            for n in sizes
        ]
        + [whole((8, 128))],
        out_shape=[
            space((n, colours, two, spins, rows, count), jnp.bfloat16)
            for n, space in zip(sizes, (pltpu.HBM, pltpu.VMEM))
        ]
        + [TOKEN],
        scratch_shapes=[pltpu.VMEM((slices, rows, STEP), jnp.bfloat16)],
        compiler_params=pltpu.CompilerParams(vmem_limit_bytes=LOW_LIMIT),
        cost_estimate=TINY,
        name="relayout_low",
    )(stay(low), after)
    turned = [t.reshape(t.shape[0], colours, two * spins * rows, count) for t in turned]
    return turned, token


def contract_body(by_part, blocks, based, added, pat_ref, cos_ref, sin_ref, own_ref, oth_ref, *refs):
    highs, refs = refs[: len(blocks)], refs[len(blocks) :]
    base_ref, refs = (refs[0], refs[1:]) if based else (None, refs)
    adds, outs = refs[:added], refs[1 + added : -2]
    token_ref, acc_ref = refs[-2:]
    token_ref[...] = jnp.zeros_like(token_ref)
    n_moms, count = cos_ref.shape
    x, _, _ = coords()
    acc_ref[...] = jnp.zeros_like(acc_ref)

    def one(colour, carry):
        total = None
        for j in range(0, count, STEP):
            cut = pl.ds(j, STEP)
            rows = []
            for high_ref in highs:
                real = high_ref[0, 0, colour, :, cut].astype(jnp.float32)
                imag = high_ref[0, 1, colour, :, cut].astype(jnp.float32)
                reals, imags = [], []
                for p in range(n_moms):
                    cosine = cos_ref[p : p + 1, cut]
                    sine = sin_ref[p : p + 1, cut]
                    reals.append((real * cosine - imag * sine).astype(jnp.bfloat16))
                    imags.append((real * sine + imag * cosine).astype(jnp.bfloat16))
                rows += reals + imags
            phased = jnp.concatenate(rows, 0)
            low = jnp.concatenate([own_ref[0, colour, :, cut], oth_ref[0, colour, :, cut]], 0)
            part = lax.dot_general(
                low, phased, (((1,), (1,)), ((), ())), preferred_element_type=jnp.float32
            )
            total = part if total is None else total + part
        acc_ref[...] += total
        return carry

    lax.fori_loop(0, 3, one, 0)
    half = 128

    def put(k, block, result):
        for add in adds:
            result = result + add[add.shape[0] - 1, k, block].astype(jnp.float32)
        if by_part:
            outs[k // 2][k % 2, 0, block] = result.astype(outs[k // 2].dtype)
        else:
            outs[0][0, k, block] = result.astype(outs[0].dtype)

    if based:
        for k in range(NX):
            put(k, 0, base_ref[0, k, 0])
    for place, block in enumerate(blocks):
        base = place * 256
        pattern = pat_ref[0:1, block * half : block * half + half]
        is_spin = [jnp.broadcast_to(pattern == a, (16, half)) for a in range(4)]
        low_pair = pattern < 2
        odd = jnp.logical_or(pattern == 1, pattern == 3)
        mesons = [[], [], [], []]
        for owner in range(2):
            over = []
            for s in range(4):
                u0 = slice(owner * 128 + s * 16, owner * 128 + s * 16 + 16)
                u1 = slice(owner * 128 + s * 16 + 64, owner * 128 + s * 16 + 80)
                r0, r1 = slice(base, base + half), slice(base + half, base + 2 * half)
                over.append((acc_ref[u0, r0] + acc_ref[u1, r1], acc_ref[u1, r0] - acc_ref[u0, r1]))
            for g in range(4):
                picked = []
                for u in range(2):
                    value = over[PARTNER[g][3]][u]
                    for a in range(3):
                        value = jnp.where(is_spin[a], over[PARTNER[g][a]][u], value)
                    picked.append(value)
                re, im = picked
                if g == 2:
                    re, im = jnp.where(low_pair, -im, im), jnp.where(low_pair, re, -re)
                if g == 3:
                    re, im = jnp.where(odd, re, -re), jnp.where(odd, im, -im)
                mesons[g] += [re, im]
        stacked = [jnp.concatenate(m, 0) for m in mesons]
        lane = lax.broadcasted_iota(jnp.int32, stacked[0].shape, 1) // 32
        for k in range(NX):
            group = x ^ OWNERS[k]
            result = None
            for g in range(4):
                turned = pltpu.roll(stacked[g], lax.rem(g - group + NX, NX) * 32, 1)
                result = turned if result is None else jnp.where(lane == g, turned, result)
            put(k, block, result)


def contract(tables, lows, own, received, first, by_part, sent, after, limit, adds=(), base=None):
    colours, rows, count = lows[0].shape[1:]
    highs = [h for h in (own, received) if h is not None]
    blocks = tuple(b for b, h in enumerate((own, received)) if h is not None)
    number = highs[0].shape[0]
    unit = (1 if received is None else 2, 64, 128)
    if by_part:
        shapes = [
            jax.ShapeDtypeStruct((2, number) + unit, sent),
            jax.ShapeDtypeStruct((2, number) + unit, jnp.float32),
        ]
        out_specs = [pl.BlockSpec((2, 1) + unit, lambda i: (0, i, 0, 0, 0))] * 2
    else:
        shapes = [jax.ShapeDtypeStruct((number, NX) + unit, sent)]
        out_specs = [pl.BlockSpec((1, NX) + unit, lambda i: (i, 0, 0, 0, 0))]
    high_spec = pl.BlockSpec((1, 2, colours, 16, count), lambda i: (i, 0, 0, 0, 0))
    low_spec = pl.BlockSpec((1, colours, rows, count), lambda i: (first + i, 0, 0, 0))
    extra = list(adds) if base is None else [base, *adds]
    return pl.pallas_call(
        functools.partial(contract_body, by_part, blocks, base is not None, len(adds)),
        grid=(number,),
        in_specs=[whole(t.shape) for t in tables]
        + [low_spec, low_spec]
        + [high_spec] * len(highs)
        + [whole(a.shape) for a in extra]
        + [whole((8, 128))],
        out_specs=out_specs + [whole((8, 128))],
        out_shape=shapes + [TOKEN],
        scratch_shapes=[pltpu.VMEM((256, 256 * len(highs)), jnp.float32)],
        compiler_params=pltpu.CompilerParams(vmem_limit_bytes=limit),
        cost_estimate=TINY,
        name=f"contract_{first}_{number}",
    )(*tables, *lows, *highs, *extra, after)


def fold_body(number, *refs):
    parts, (first_ref, second_ref, token_ref) = refs[:number], refs[-3:]
    half = parts[0].shape[0] // 2
    for out_ref, cut in ((first_ref, slice(0, half)), (second_ref, slice(half, 2 * half))):
        total = None
        for part in parts:
            value = part[cut].astype(jnp.float32)
            total = value if total is None else total + value
        out_ref[...] = total.astype(out_ref.dtype)
    token_ref[...] = jnp.zeros_like(token_ref)


def fold(parts, sent, after):
    shape = (parts[0].shape[0] // 2,) + parts[0].shape[1:]
    return pl.pallas_call(
        functools.partial(fold_body, len(parts)),
        in_specs=[VMEM] * (len(parts) + 1),
        out_specs=[VMEM] * 3,
        out_shape=[
            jax.ShapeDtypeStruct(shape, sent),
            jax.ShapeDtypeStruct(shape, jnp.float32),
            TOKEN,
        ],
        compiler_params=SMALL,
        cost_estimate=TINY,
        name="fold",
    )(*parts, after)


def plus_body(number, *refs):
    parts, out_ref, token_ref = refs[:number], refs[-2], refs[-1]
    total = None
    for part in parts:
        value = part[: out_ref.shape[0]].astype(jnp.float32)
        total = value if total is None else total + value
    out_ref[...] = total.astype(out_ref.dtype)
    token_ref[...] = jnp.zeros_like(token_ref)


def plus(parts, sent, after):
    length = min(part.shape[0] for part in parts)
    return pl.pallas_call(
        functools.partial(plus_body, len(parts)),
        in_specs=[VMEM] * (len(parts) + 1),
        out_specs=[VMEM] * 2,
        out_shape=[jax.ShapeDtypeStruct((length,) + parts[0].shape[1:], sent), TOKEN],
        compiler_params=SMALL,
        cost_estimate=TINY,
        name="plus",
    )(*parts, after)


def finish_body(kept_ref, last_ref, across_ref, mine_ref, other_ref):
    for out_ref, rows in ((mine_ref, slice(0, 32)), (other_ref, slice(32, 64))):
        out_ref[...] = kept_ref[0, :, rows] + last_ref[0, :, rows].astype(jnp.float32) + across_ref[0, :, rows]


def finish(kept, last, across):
    return pl.pallas_call(
        finish_body,
        in_specs=[VMEM] * 3,
        out_specs=[VMEM] * 2,
        out_shape=[jax.ShapeDtypeStruct((2, 32, 128), jnp.float32)] * 2,
        compiler_params=SMALL,
        cost_estimate=TINY,
        name="finish",
    )(kept, last, across)


def assemble_body(mine_ref, other_ref, out_ref):
    mode = lax.axis_index("mode")
    blocks = [mode, mode ^ 2, mode ^ 1, mode ^ 3]
    lane = lax.broadcasted_iota(jnp.int32, (32, 128), 1) // 16
    held = [mine_ref[0], mine_ref[1], other_ref[0], other_ref[1]]
    for g in range(4):
        for p in range(2):
            result = None
            for values, block in zip(held, blocks):
                shift = lax.rem(block * 16 - (g * 32 + p * 16) + 128, 128)
                turned = pltpu.roll(values, shift, 1)
                result = turned if result is None else jnp.where(lane == block, turned, result)
            for u in range(2):
                out_ref[g, u, p] = result[u * 16 : u * 16 + 16, :64]


def assemble(pieces):
    return pl.pallas_call(
        assemble_body,
        out_shape=jax.ShapeDtypeStruct((4, 2, 2, 16, 64), jnp.float32),
        compiler_params=SMALL,
        cost_estimate=TINY,
        name="assemble",
    )(*pieces)


def phase_tables(momenta, first_site, count):
    sites = first_site + jnp.arange(count, dtype=jnp.int32)
    coords = jnp.stack([sites % 32, sites // 32 % 32, sites // 1024])
    turns = jnp.sum(momenta[:, :, None] * coords[None, :, :], axis=1)
    angles = turns.astype(jnp.float32) * (2.0 * math.pi / 96.0)
    return jnp.cos(angles), jnp.sin(angles)


def body(low_modes, high_modes, pattern, momenta):
    count = low_modes.shape[-1]
    my_mode = lax.axis_index("mode")
    wide, narrow = jnp.float32, jnp.bfloat16
    *high, token = relayout_high(high_modes, (2, 2, 2, 1, 1))
    arrived = [flip(chunk, 2) for chunk in high]
    gated, token = lax.optimization_barrier((low_modes, token))
    low_oth = flip(gated, 1)
    low_own, token = relayout_low(low_modes, token, (4, 4))
    low_oth, token = relayout_low(low_oth, token, (4, 4))
    many, few = zip(low_own, low_oth)
    many = [stay(a) for a in many]
    cosines, sines = phase_tables(momenta, lax.axis_index("site") * count, count)

    def lanes(block):
        part = lax.dynamic_slice_in_dim(pattern, block * 16, 16, 0)
        return jnp.broadcast_to(jnp.tile(part, 8)[None, :], (8, 128))

    tables = (jnp.concatenate([lanes(my_mode), lanes(my_mode ^ 2)], 1), cosines, sines)
    away, token = contract(
        tables, many, high[0], arrived[0], 0, False, narrow, token, MANY_LIMIT
    )
    far_got = trade(away, 1, 0, 0)
    far, token = contract(
        tables, many, high[1], arrived[1], 2, False, wide, token, MANY_LIMIT
    )
    away, far, token = fold((far, far_got), narrow, token)
    far_got = trade(away, 3, 0, 0)
    base, token = contract(tables, few, high[3], None, 2, False, wide, token, FEW_LIMIT)
    away, far, token = fold((far[0], far_got[0]), narrow, token)
    far_got = trade(away, 0, 0, 1)
    last_base, token = contract(tables, few, high[4], None, 3, False, wide, token, FEW_LIMIT)
    away, far, token = fold((far, far_got), narrow, token)
    far_got = trade(away, 0, 0, 3)
    away, token = contract(
        tables, few, high[2], arrived[2], 0, False, narrow, token, FEW_LIMIT
    )
    near_got = trade(away, 1, 0, 0)
    near, token = contract(
        tables, few, None, arrived[3], 2, False, wide, token, FEW_LIMIT, (), base
    )
    away, token = plus((far, far_got), wide, token)
    across = trade(away, 0, 1, 0)
    away, token = plus((near, near_got), narrow, token)
    near_last = trade(away, 3, 0, 0)
    near, token = contract(
        tables, few, None, arrived[4], 3, False, wide, token, FEW_LIMIT, (near_got,), last_base
    )
    away, near, token = fold((near[0], near_last[0]), narrow, token)
    last_got = trade(away, 0, 0, 1)
    away, near, token = fold((near, last_got), narrow, token)
    last_got = trade(away, 0, 0, 3)
    mine, other = finish(near, last_got, across)
    pieces = (mine, flip(other, 1))
    return jnp.transpose(assemble(pieces), (0, 1, 2, 4, 3))


def solution(mesh):
    placed = (
        P("mode", None, None, None, None, "site"),
        P("mode", None, None, None, "site"),
        P(),
        P(),
    )
    return jax.shard_map(
        body,
        mesh=mesh,
        in_specs=placed,
        out_specs=P(None, None, "site", None, "mode"),
        check_vma=False,
    )
```
